256 devices in a mesh: depth: 8 (over z_hi, core), eta: 32 (over x, z_lo, y).
Axes of the slice: x: 4, y: 4, z: 8 (z_hi: 4, z_lo: 2; z = z_hi * 2 + z_lo), core: 2. Of those that a mesh axis runs over, the one named last changes fastest.
Arguments:
- field_in: bfloat16 [16, 128, 32, 2048], P('depth', 'eta'), may hold values from -6 to 6
- grad_out: bfloat16 [16, 128, 32, 2048], P('depth', 'eta'), may hold values from -6 to 6
- spectral_weight: bfloat16 [2, 64, 64, 1024], P(None, 'eta'), may hold values from -0.75 to 0.75
- mlp_in: bfloat16 [32, 64], replicated, may hold values from -1 to 1
- mlp_bias: float32 [64], replicated, may hold values from -3 to 3
- mlp_out: bfloat16 [64, 32], replicated, may hold values from -0.75 to 0.75
Outputs:
- grad_in: float32 [16, 128, 32, 2048], P('depth', 'eta')
- grad_spectral: float32 [2, 64, 64, 1024], P(None, 'eta', 'depth')
- grad_mlp_in: float32 [32, 64], replicated
- grad_mlp_out: float32 [64, 32], replicated
- grad_mlp_bias: float32 [64], replicated
The draws below stay inside these ranges and needn't reach their ends.
All inputs are finite; a program needn't handle non-finite values.
Results may differ from the reference program's by a relative error of at most 0.0087.
Values may be sent and summed in bfloat16 or wider, within the bound.
A program may use at most 128 MiB of HBM per device.

```python
import math
import jax
import jax.numpy as jnp
from jax import lax

CH = 32
HID = 64
NP = 2048
MP = 64
ME = 64
NE = 128
DEPTH = 16


def block_scale(stream_key, extent, split, smallest, top_value):
    factor_of, own = 1.0, jax.random.fold_in(stream_key, 6)
    for axis_at, blocks in split:
        heights = jnp.exp(jax.random.uniform(jax.random.fold_in(own, axis_at), (blocks,), jnp.float32, smallest / len(split), top_value / len(split)))
        factor_of = factor_of * jnp.repeat(heights, extent[axis_at] // blocks).reshape([-1 if axis == axis_at else 1 for axis in range(len(extent))])
    return factor_of


def normal_values(own_key, extent, width, reach, shards=(), kind=jnp.bfloat16):
    loudness = block_scale(own_key, extent, shards, -0.22, 0.18) if shards else 1.0
    result = jax.random.normal(own_key, extent, jnp.float32) * width * loudness
    return jnp.minimum(jnp.maximum(result, -reach), reach).astype(kind)


def setup_inputs(seed: int = 0) -> dict:
    keys = jax.random.split(jax.random.key(seed), 7)
    field_in = normal_values(keys[0], (DEPTH, NE, CH, NP), 1.0, 6.0, ((0, 8), (1, 32)))
    grad_out = normal_values(keys[1], (DEPTH, NE, CH, NP), 1.0, 6.0, ((0, 8), (1, 32)))
    spectral_weight = normal_values(keys[2], (2, MP, ME, CH * CH), (2 * CH) ** -0.5, 0.75, ((1, 32),))
    mlp_in = normal_values(keys[3], (CH, HID), CH ** -0.5, 1.0)
    mlp_bias = normal_values(keys[4], (HID,), 0.5, 3.0, (), jnp.float32)
    mlp_out = normal_values(keys[5], (HID, CH), HID ** -0.5, 0.75)
    return {"field_in": field_in, "grad_out": grad_out, "spectral_weight": spectral_weight, "mlp_in": mlp_in, "mlp_bias": mlp_bias, "mlp_out": mlp_out}


def phi_tables(n_phi, n_modes):
    cells = jnp.arange(n_phi, dtype=jnp.int32)
    index = jnp.arange(n_modes, dtype=jnp.int32)
    freq = jnp.where(index < n_modes // 2, index, n_phi - n_modes + index)
    theta = 2.0 * math.pi / n_phi * (cells[:, None] * freq[None, :] % n_phi).astype(jnp.float32)
    pairs = jnp.stack([jnp.cos(theta), -jnp.sin(theta)], axis=-1).reshape(n_phi, 2 * n_modes)
    forward = (pairs / math.sqrt(n_phi)).astype(jnp.bfloat16)
    inverse = (pairs.T / math.sqrt(n_modes)).astype(jnp.bfloat16)
    return (forward, inverse)

def eta_tables(n_eta, n_modes, start, count):
    cells = start + jnp.arange(count, dtype=jnp.int32)
    index = jnp.arange(n_modes, dtype=jnp.int32)
    phase = 2.0 * math.pi / n_eta * (cells[:, None] * index[None, :] % n_eta).astype(jnp.float32)
    cosine = jnp.cos(phase)
    sine = jnp.sin(phase)
    return ((cosine / math.sqrt(n_eta)).astype(jnp.bfloat16), (sine / math.sqrt(n_eta)).astype(jnp.bfloat16), cosine.T / math.sqrt(n_modes), sine.T / math.sqrt(n_modes))

def gelu_slope(value):
    normal_cdf = 0.5 * (1.0 + lax.erf(value / math.sqrt(2.0)))
    return normal_cdf + value * jnp.exp(-0.5 * value * value) / math.sqrt(2.0 * math.pi)

def eta_forward(spectra, eta_cos, eta_sin):
    layers, cells, chans, twice = spectra.shape
    parts = spectra.astype(jnp.float32).reshape(layers, cells, chans, twice // 2, 2)
    real_part = parts[..., 0]
    imag_part = parts[..., 1]
    cosf = eta_cos.astype(jnp.float32)
    sinf = eta_sin.astype(jnp.float32)
    hp = lax.Precision.HIGHEST
    zr = jnp.einsum('decj,em->jdmc', real_part, cosf, precision=hp) + jnp.einsum('decj,em->jdmc', imag_part, sinf, precision=hp)
    zi = jnp.einsum('decj,em->jdmc', imag_part, cosf, precision=hp) - jnp.einsum('decj,em->jdmc', real_part, sinf, precision=hp)
    return jnp.stack([zr, zi], axis=2)

def eta_inverse(modes, inv_cos, inv_sin):
    hp = lax.Precision.HIGHEST
    vr = modes[:, :, 0]
    vi = modes[:, :, 1]
    wr = jnp.einsum('jdmc,me->decj', vr, inv_cos, precision=hp) - jnp.einsum('jdmc,me->decj', vi, inv_sin, precision=hp)
    wi = jnp.einsum('jdmc,me->decj', vr, inv_sin, precision=hp) + jnp.einsum('jdmc,me->decj', vi, inv_cos, precision=hp)
    layers, cells, chans, count = wr.shape
    return jnp.stack([wr, wi], axis=-1).reshape(layers, cells, chans, 2 * count).astype(jnp.bfloat16)

def reference(field_in, grad_out, spectral_weight, mlp_in, mlp_bias, mlp_out):
    hp = lax.Precision.HIGHEST
    phi_fwd, phi_inv = phi_tables(NP, MP)
    eta_cos, eta_sin, inv_cos, inv_sin = eta_tables(NE, ME, 0, NE)
    weights = spectral_weight.astype(jnp.float32).reshape(2, MP, ME, CH, CH)
    rr = weights[0]
    ri = weights[1]
    w_in = mlp_in.astype(jnp.float32)
    w_out = mlp_out.astype(jnp.float32)

    def layer(carry, inputs):
        grad_r, grad_i, acc_in, acc_out, acc_bias = carry
        field = inputs[0][None]
        cotan = inputs[1][None]
        xp = jnp.dot(field, phi_fwd, preferred_element_type=jnp.float32).astype(jnp.bfloat16)
        zx = eta_forward(xp, eta_cos, eta_sin)
        zr = zx[:, :, 0]
        zi = zx[:, :, 1]
        vr = jnp.einsum('kdmc,kmco->kdmo', zr, rr, precision=hp) - jnp.einsum('kdmc,kmco->kdmo', zi, ri, precision=hp)
        vi = jnp.einsum('kdmc,kmco->kdmo', zr, ri, precision=hp) + jnp.einsum('kdmc,kmco->kdmo', zi, rr, precision=hp)
        wx = eta_inverse(jnp.stack([vr, vi], axis=2), inv_cos, inv_sin)
        spectral = jnp.dot(wx, phi_inv, preferred_element_type=jnp.float32)
        field32 = field.astype(jnp.float32)
        hidden_pre = jnp.einsum('decp,ch->dehp', field32, w_in) + mlp_bias[None, None, :, None]
        hidden = jax.nn.gelu(hidden_pre, approximate=False).astype(jnp.bfloat16)
        pre = spectral + jnp.einsum('dehp,hc->decp', hidden.astype(jnp.float32), w_out)
        gpre = (cotan.astype(jnp.float32) * gelu_slope(pre)).astype(jnp.bfloat16)
        gp = jnp.dot(gpre, phi_fwd, preferred_element_type=jnp.float32).astype(jnp.bfloat16)
        zg = eta_forward(gp, eta_cos, eta_sin)
        gr = zg[:, :, 0]
        gi = zg[:, :, 1]
        grad_r = grad_r + jnp.einsum('kdmc,kdmo->kmco', zr, gr, precision=hp) + jnp.einsum('kdmc,kdmo->kmco', zi, gi, precision=hp)
        grad_i = grad_i + jnp.einsum('kdmc,kdmo->kmco', zr, gi, precision=hp) - jnp.einsum('kdmc,kdmo->kmco', zi, gr, precision=hp)
        br = jnp.einsum('kdmo,kmco->kdmc', gr, rr, precision=hp) + jnp.einsum('kdmo,kmco->kdmc', gi, ri, precision=hp)
        bi = jnp.einsum('kdmo,kmco->kdmc', gi, rr, precision=hp) - jnp.einsum('kdmo,kmco->kdmc', gr, ri, precision=hp)
        wb = eta_inverse(jnp.stack([br, bi], axis=2), inv_cos, inv_sin)
        back_spec = jnp.dot(wb, phi_inv, preferred_element_type=jnp.float32)
        gpre32 = gpre.astype(jnp.float32)
        hidden_grad = jnp.einsum('decp,hc->dehp', gpre32, w_out) * gelu_slope(hidden_pre)
        hidden_gb = hidden_grad.astype(jnp.bfloat16).astype(jnp.float32)
        grad_field = cotan.astype(jnp.float32) + back_spec + jnp.einsum('dehp,ch->decp', hidden_gb, w_in)
        acc_in = acc_in + jnp.einsum('decp,dehp->ch', field32, hidden_gb)
        acc_out = acc_out + jnp.einsum('dehp,decp->hc', hidden.astype(jnp.float32), gpre32)
        acc_bias = acc_bias + lax.optimization_barrier(jnp.sum(hidden_grad, axis=(0, 1, 3)))
        return ((grad_r, grad_i, acc_in, acc_out, acc_bias), grad_field[0])
    start = (jnp.zeros((MP, ME, CH, CH), jnp.float32), jnp.zeros((MP, ME, CH, CH), jnp.float32), jnp.zeros((CH, HID), jnp.float32), jnp.zeros((HID, CH), jnp.float32), jnp.zeros((HID,), jnp.float32))
    final, grad_in = lax.scan(layer, start, (field_in, grad_out))
    grad_r, grad_i, acc_in, acc_out, acc_bias = final
    factor = math.sqrt(NP * NE / (MP * ME))
    grad_spectral = (jnp.stack([grad_r, grad_i], axis=0) * factor).reshape(2, MP, ME, CH * CH)
    norm = 1.0 / math.sqrt(DEPTH * NE * NP)
    return (grad_in, grad_spectral, acc_in * norm, acc_out * norm, acc_bias * norm)
```

```python
import functools
import math

import jax
import jax.numpy as jnp
import ml_dtypes
import numpy as np
from jax import lax
from jax.experimental import pallas as pl
from jax.experimental.pallas import tpu as pltpu
from jax.sharding import PartitionSpec as P

F32 = jnp.float32
BF16 = jnp.bfloat16
MESH = pl.DeviceIdType.MESH


def bf(table):
    return table.astype(np.float32).astype(ml_dtypes.bfloat16)


def phi_table(n_phi, n_modes):
    owners = n_modes // 2
    mode = 2 * np.arange(owners)[None, :] + np.arange(2)[:, None]
    freq = np.where(mode < n_modes // 2, mode, n_phi - n_modes + mode)
    theta = 2.0 * np.pi / n_phi * ((freq[:, :, None] * np.arange(n_phi)) % n_phi)
    pairs = np.stack([np.cos(theta), -np.sin(theta)], axis=1).reshape(4 * owners, n_phi)
    return bf(pairs / math.sqrt(n_phi)), bf(pairs / math.sqrt(n_modes))


def eta_tables(n_eta, n_modes, owners):
    j, hi, lo = np.meshgrid(np.arange(owners), np.arange(2), np.arange(2), indexing="ij")
    cell = 4 * j + 2 * hi + lo
    phase = 2.0 * np.pi / n_eta * ((cell[..., None] * np.arange(n_modes)) % n_eta)
    cosine, sine = np.cos(phase), np.sin(phase)
    fwd = np.zeros((2, owners, 2, 2, 2, 2, 2, n_modes))
    inv = np.zeros((owners, 2, 2, 2, 2, 2, 2, n_modes))
    for low in range(2):
        c, s = cosine[:, :, low], sine[:, :, low]
        for kk in range(2):
            fwd[low, :, kk, 0, :, 0, kk] = c
            fwd[low, :, kk, 1, :, 0, kk] = s
            fwd[low, :, kk, 0, :, 1, kk] = -s
            fwd[low, :, kk, 1, :, 1, kk] = c
            inv[:, kk, 0, :, low, 0, kk] = c
            inv[:, kk, 0, :, low, 1, kk] = -s
            inv[:, kk, 1, :, low, 0, kk] = s
            inv[:, kk, 1, :, low, 1, kk] = c
    fwd = fwd.reshape(2 * 8 * owners, 4 * n_modes) / math.sqrt(n_eta)
    inv = inv.reshape(8 * owners, 8 * n_modes) / math.sqrt(n_modes)
    return bf(fwd), bf(inv)


def nn(a, b):
    return lax.dot_general(a, b, (((1,), (0,)), ((), ())), preferred_element_type=F32)


def nt(a, b):
    return lax.dot_general(a, b, (((1,), (1,)), ((), ())), preferred_element_type=F32)


def cdf_and_density(v):
    cdf = 0.5 + 0.5 * lax.erf(v * (1.0 / math.sqrt(2.0)))
    density = jnp.exp(-0.5 * v * v) * (1.0 / math.sqrt(2.0 * math.pi))
    return cdf, density


def eta_order(x):
    blocks = [x[b * 32 : (b + 1) * 32] for b in range(8)]
    return jnp.concatenate([blocks[d * 4 + hi * 2 + lo] for hi in range(2) for lo in range(2) for d in range(2)], axis=0)


def cell_order(x):
    blocks = [x[b * 32 : (b + 1) * 32] for b in range(8)]
    return jnp.concatenate([blocks[hi * 4 + lo * 2 + d] for d in range(2) for hi in range(2) for lo in range(2)], axis=0)


def kernel(
    n_dep,
    n_eta,
    chunk,
    factor,
    norm,
    field_hbm,
    cotan_hbm,
    weight_hbm,
    mlp_in,
    mlp_bias,
    mlp_out,
    fwd_hbm,
    inv_hbm,
    efwd_hbm,
    einv_hbm,
    gin_hbm,
    gspec,
    out_in,
    out_out,
    out_bias,
    field,
    cotan,
    weight,
    tfwd,
    tinv,
    efwd,
    einv,
    hid,
    slope,
    part,
    gpre,
    w_all,
    m_up,
    m_down,
    m_outt,
    m_out,
    bias_col,
    rt,
    rt2,
    zbuf,
    vsend,
    sends,
    recvs,
    dsend,
    drecv,
    xexp,
    gexp,
    asend,
    arecv,
    bsend,
    brecv,
    csend,
    crecv,
    load_sem,
    out_sem,
    send_sem,
    recv_sem,
):
    dep = lax.axis_index("depth")
    eta = lax.axis_index("eta")
    n_phi = field.shape[1]
    n_chunks = n_phi // chunk

    barrier = pltpu.get_barrier_semaphore()

    def greet_eta(s, c):
        pl.semaphore_signal(barrier, inc=1, device_id=(dep, lax.rem(eta + s, n_eta)), device_id_type=MESH)
        return c

    def greet_dep(s, c):
        pl.semaphore_signal(barrier, inc=1, device_id=(lax.rem(dep + s, n_dep), eta), device_id_type=MESH)
        return c

    loads = [
        pltpu.make_async_copy(src, dst, load_sem.at[n])
        for n, (src, dst) in enumerate(
            (
                (field_hbm, field),
                (fwd_hbm, tfwd),
                (efwd_hbm, efwd),
                (einv_hbm, einv),
                (weight_hbm, weight),
                (inv_hbm, tinv),
                (cotan_hbm, cotan),
            )
        )
    ]
    for copy in loads:
        copy.start()
    lax.fori_loop(1, n_eta, greet_eta, 0)
    lax.fori_loop(1, n_dep, greet_dep, 0)

    def eta_start(n, send, recv):
        def step(s, c):
            peer = lax.rem(eta + s, n_eta)
            pltpu.make_async_remote_copy(
                src_ref=send.at[pl.ds(pl.multiple_of(peer * 8, 8), 8)],
                dst_ref=recv.at[pl.ds(pl.multiple_of(eta * 8, 8), 8)],
                send_sem=send_sem.at[n],
                recv_sem=recv_sem.at[n],
                device_id=(dep, peer),
                device_id_type=MESH,
            ).start()
            return c

        lax.fori_loop(1, n_eta, step, 0)
        own = pl.ds(pl.multiple_of(eta * 8, 8), 8)
        recv[own, :] = send[own, :]

    def eta_wait(n, recv):
        rows = pl.ds(0, 8 * (n_eta - 1))
        pltpu.make_async_copy(recv.at[rows], recv.at[rows], recv_sem.at[n]).wait()

    def eta_sent(n, send):
        rows = pl.ds(0, 8 * (n_eta - 1))
        pltpu.make_async_copy(send.at[rows], send.at[rows], send_sem.at[n]).wait()

    def gather_start(n, axis, block, recv):
        me, count = (dep, n_dep) if axis == "depth" else (eta, n_eta)

        def step(s, c):
            peer = lax.rem(me + s, count)
            pltpu.make_async_remote_copy(
                src_ref=block,
                dst_ref=recv.at[me],
                send_sem=send_sem.at[n],
                recv_sem=recv_sem.at[n],
                device_id=(peer, eta) if axis == "depth" else (dep, peer),
                device_id_type=MESH,
            ).start()
            return c

        lax.fori_loop(1, count, step, 0)
        recv[me] = block[...]

    def blocks_wait(sem, recv, count):
        some = pl.ds(0, count - 1)
        pltpu.make_async_copy(recv.at[some], recv.at[some], sem).wait()

    def phi_forward(x, send):
        spectra = nt(tfwd[...], eta_order(x))
        for q in range(4):
            for hi in range(2):
                send[pl.ds(q * 2 + hi, n_eta, stride=8), :] = spectra[
                    q * n_eta : (q + 1) * n_eta, hi * 128 : (hi + 1) * 128
                ]

    def eta_forward(recv):
        xt = recv[...].T.astype(BF16)
        half = 8 * n_eta
        return nn(xt[0:64], efwd[0:half, :]) + nn(xt[64:128], efwd[half:, :])

    def eta_inverse(real, imag, send):
        v = jnp.concatenate([real, imag], axis=1).astype(BF16)
        zero = jnp.zeros_like(v)
        both = jnp.concatenate(
            [jnp.concatenate([v, zero], axis=1), jnp.concatenate([zero, v], axis=1)], axis=0
        )
        send[...] = nt(einv[...], both)

    def phi_inverse_lhs(recv):
        halves = []
        for hi in range(2):
            rows = [recv[pl.ds(q * 2 + hi, n_eta, stride=8), :] for q in range(4)]
            halves.append(jnp.concatenate(rows, axis=0).T)
        w_all[...] = cell_order(jnp.concatenate(halves, axis=0)).astype(BF16)

    def tile_rows(x):
        return jnp.concatenate([x] * 4, axis=0)

    spread_in = (
        lax.broadcasted_iota(jnp.int32, (64, 256), 0) == lax.rem(lax.broadcasted_iota(jnp.int32, (64, 256), 1), 64)
    ).astype(F32).astype(BF16)
    spread_out = (
        lax.broadcasted_iota(jnp.int32, (32, 128), 0) == lax.rem(lax.broadcasted_iota(jnp.int32, (32, 128), 1), 32)
    ).astype(F32).astype(BF16)
    in_tiled = tile_rows(nn(mlp_in[...], spread_in))
    keep = (
        lax.broadcasted_iota(jnp.int32, (128, 256), 0) // 32 == lax.broadcasted_iota(jnp.int32, (128, 256), 1) // 64
    )
    down = jnp.where(keep, in_tiled, 0.0)
    m_down[...] = down.astype(BF16)
    m_up[...] = down.T.astype(BF16)
    out_tiled = tile_rows(nn(mlp_out[...], spread_out))
    keep_out = (
        lax.broadcasted_iota(jnp.int32, (256, 128), 0) // 64 == lax.broadcasted_iota(jnp.int32, (256, 128), 1) // 32
    )
    outm = jnp.where(keep_out, out_tiled, 0.0)
    m_out[...] = outm.astype(BF16)
    m_outt[...] = outm.T.astype(BF16)
    diagonal = lax.broadcasted_iota(jnp.int32, (64, 64), 0) == lax.broadcasted_iota(jnp.int32, (64, 64), 1)
    column = jnp.sum(jnp.where(diagonal, mlp_bias[...], 0.0), axis=1, keepdims=True)
    bias_col[...] = jnp.broadcast_to(tile_rows(column), (256, 128))

    loads[0].wait()
    loads[1].wait()
    phi_forward(field[...], sends.at[0])
    pl.semaphore_wait(barrier, n_eta + n_dep - 2)
    eta_start(0, sends.at[0], recvs.at[0])

    def mlp_forward(g):
        def body(i, c):
            cols = pl.ds(pl.multiple_of(i * chunk, chunk), chunk)
            pre = nn(m_up[...], field[g * 128 : (g + 1) * 128, cols])
            pre = pre + jnp.concatenate([bias_col[...]] * (chunk // 128), axis=1)
            cdf, density = cdf_and_density(pre)
            hidden = (pre * cdf).astype(BF16)
            hid[g * 256 : (g + 1) * 256, cols] = hidden
            slope[g * 256 : (g + 1) * 256, cols] = (cdf + pre * density).astype(BF16)
            part[g * 128 : (g + 1) * 128, cols] = nn(m_outt[...], hidden)
            return c

        lax.fori_loop(0, n_chunks, body, 0)

    loads[4].wait()
    for ri in range(2):
        rt[ri] = weight[ri * 128 : (ri + 1) * 128, :].astype(F32).T
    mlp_forward(0)

    loads[2].wait()
    loads[3].wait()
    eta_wait(0, recvs.at[0])
    zx = eta_forward(recvs.at[0])
    for ri in range(2):
        zbuf[ri] = zx[:, ri * 128 : (ri + 1) * 128]
    dsend_x = zx

    def mix(table, sign):
        real = [jnp.zeros((32, 128), F32) for _ in range(2)]
        imag = [jnp.zeros((32, 128), F32) for _ in range(2)]
        for c in range(32):
            wr = table[0, c * 32 : (c + 1) * 32, :]
            wi = table[1, c * 32 : (c + 1) * 32, :]
            for d in range(2):
                zr = zbuf[0, d * 32 + c : d * 32 + c + 1, :]
                zi = zbuf[1, d * 32 + c : d * 32 + c + 1, :]
                real[d] = real[d] + (zr * wr - sign * (zi * wi))
                imag[d] = imag[d] + (zi * wr + sign * (zr * wi))
        return jnp.concatenate(real, axis=0), jnp.concatenate(imag, axis=0)

    vr, vi = mix(rt, 1.0)
    eta_inverse(vr, vi, sends.at[1])
    eta_start(1, sends.at[1], recvs.at[1])

    dsend[:, :, 0:64] = dsend_x.T.reshape(4, 64, 64)
    mlp_forward(1)
    for ri in range(2):
        for o in range(32):
            rt2[ri, o * 32 : (o + 1) * 32, :] = rt[ri, pl.ds(o, 32, stride=32), :]

    loads[5].wait()
    loads[6].wait()
    eta_wait(1, recvs.at[1])
    phi_inverse_lhs(recvs.at[1])

    def pre_body(i, c):
        cols = pl.ds(pl.multiple_of(i * chunk, chunk), chunk)
        pre = nn(w_all[...], tinv[:, cols]) + part[:, cols]
        cdf, density = cdf_and_density(pre)
        gpre[:, cols] = (cotan[:, cols].astype(F32) * (cdf + pre * density)).astype(BF16)
        return c

    lax.fori_loop(0, n_chunks, pre_body, 0)
    phi_forward(gpre[...], sends.at[2])
    eta_start(2, sends.at[2], recvs.at[2])

    def mlp_backward(g):
        def body(i, c):
            cols = pl.ds(pl.multiple_of(i * chunk, chunk), chunk)
            grad = nn(m_out[...], gpre[g * 128 : (g + 1) * 128, cols])
            grad = (grad * slope[g * 256 : (g + 1) * 256, cols].astype(F32)).astype(BF16)
            slope[g * 256 : (g + 1) * 256, cols] = grad
            rows = slice(g * 128, (g + 1) * 128)
            part[rows, cols] = cotan[rows, cols].astype(F32) + nn(m_down[...], grad)
            return c

        lax.fori_loop(0, n_chunks, body, 0)

    lane64 = lax.broadcasted_iota(jnp.int32, (64, 128), 1)
    lane32 = lax.broadcasted_iota(jnp.int32, (32, 128), 1)
    lane8 = lax.broadcasted_iota(jnp.int32, (8, 128), 1)
    sum_out = jnp.zeros((64, 128), F32)
    sum_in = jnp.zeros((32, 128), F32)
    sum_bias = jnp.zeros((8, 128), F32)
    ones = jnp.ones((8, n_phi), BF16)
    for g in range(2):
        mlp_backward(g)
        hgb = slope[g * 256 : (g + 1) * 256, :]
        by_in = nt(field[g * 128 : (g + 1) * 128, :], hgb)
        by_out = nt(hid[g * 256 : (g + 1) * 256, :], gpre[g * 128 : (g + 1) * 128, :])
        by_bias = nt(ones, hgb)
        for a in range(4):
            tile = by_in[a * 32 : (a + 1) * 32, (a // 2) * 128 : (a // 2 + 1) * 128]
            sum_in = sum_in + (pltpu.roll(tile, 64, 1) if a % 2 else tile)
            tile = by_out[a * 64 : (a + 1) * 64, :]
            turn = (64 - 32 * a) % 128
            sum_out = sum_out + (pltpu.roll(tile, turn, 1) if turn else tile)
            tile = by_bias[:, (a // 2) * 128 : (a // 2 + 1) * 128]
            sum_bias = sum_bias + (pltpu.roll(tile, 64, 1) if a % 2 else tile)
    total = jnp.where((lane64 >= 64) & (lane64 < 96), sum_out, 0.0)
    low = jnp.concatenate(
        [
            jnp.where(lane32 < 64, sum_in, 0.0),
            jnp.where(lane8 < 64, sum_bias, 0.0),
            jnp.zeros((24, 128), F32),
        ],
        axis=0,
    )
    asend[...] = (total + low).reshape(asend.shape)

    def scatter_step(s, c):
        peer = lax.rem(dep + s, n_dep)
        pltpu.make_async_remote_copy(
            src_ref=asend.at[peer],
            dst_ref=arecv.at[dep],
            send_sem=send_sem.at[4],
            recv_sem=recv_sem.at[4],
            device_id=(peer, eta),
            device_id_type=MESH,
        ).start()
        return c

    lax.fori_loop(1, n_dep, scatter_step, 0)
    arecv[dep] = asend[dep]

    eta_wait(2, recvs.at[2])
    zg = eta_forward(recvs.at[2])
    for ri in range(2):
        zbuf[ri] = zg[:, ri * 128 : (ri + 1) * 128]
    br, bi = mix(rt2, -1.0)
    eta_inverse(br, bi, sends.at[3])
    eta_start(3, sends.at[3], recvs.at[3])

    dsend[:, :, 64:128] = zg.T.reshape(4, 64, 64)
    mb = drecv.shape[2]

    def depth_step(s, c):
        peer = lax.rem(dep + s, n_dep)
        pltpu.make_async_remote_copy(
            src_ref=dsend.at[:, pl.ds(pl.multiple_of(peer * mb, mb), mb), :],
            dst_ref=drecv.at[dep],
            send_sem=send_sem.at[5],
            recv_sem=recv_sem.at[5],
            device_id=(peer, eta),
            device_id_type=MESH,
        ).start()
        return c

    lax.fori_loop(1, n_dep, depth_step, 0)
    drecv[dep] = dsend[:, pl.ds(pl.multiple_of(dep * mb, mb), mb), :]

    blocks_wait(recv_sem.at[4], arecv, n_dep)
    mine = arecv[0]
    for i in range(1, n_dep):
        mine = mine + arecv[i]
    bsend[...] = mine
    gather_start(6, "eta", bsend, brecv)

    blocks_wait(recv_sem.at[5], drecv, n_dep)
    got = drecv[...].reshape(256, 128)
    lane = lax.broadcasted_iota(jnp.int32, (256, 128), 1)
    row_c = lax.rem(lax.broadcasted_iota(jnp.int32, (128, 1024), 0), 32)
    repeat = (row_c == lax.broadcasted_iota(jnp.int32, (128, 1024), 1) // 32).astype(F32).astype(BF16)
    row_o = lax.rem(lax.broadcasted_iota(jnp.int32, (128, 128), 0), 32)
    tiled = (row_o == lax.rem(lax.broadcasted_iota(jnp.int32, (128, 128), 1), 32)).astype(F32).astype(BF16)
    for d in range(2):
        xexp[d] = nn(jnp.where(lane // 32 == d, got, 0.0).astype(BF16), repeat)
        gexp[d] = nn(jnp.where(lane // 32 == 2 + d, got, 0.0).astype(BF16), tiled)
    for kk in range(2):
        for t in range(8):
            lanes = slice(t * 128, (t + 1) * 128)
            real = jnp.zeros((mb, 128), F32)
            imag = jnp.zeros((mb, 128), F32)
            for i in range(n_dep):
                r0 = (i * 4 + kk) * mb
                r1 = (i * 4 + 2 + kk) * mb
                for d in range(2):
                    xr = xexp[d, r0 : r0 + mb, lanes]
                    xi = xexp[d, r1 : r1 + mb, lanes]
                    gr = gexp[d, r0 : r0 + mb, :]
                    gi = gexp[d, r1 : r1 + mb, :]
                    real = real + (xr * gr + xi * gi)
                    imag = imag + (xr * gi - xi * gr)
            gspec[0, kk, :, lanes] = real * factor
            gspec[1, kk, :, lanes] = imag * factor

    blocks_wait(recv_sem.at[6], brecv, n_eta)
    mine = brecv[0]
    for i in range(1, n_eta):
        mine = mine + brecv[i]
    csend[...] = mine * norm
    gather_start(7, "depth", csend, crecv)

    eta_wait(3, recvs.at[3])
    phi_inverse_lhs(recvs.at[3])

    outs = []
    for i in range(n_chunks):
        cols = pl.ds(i * chunk, chunk)
        part[:, cols] = part[:, cols] + nn(w_all[...], tinv[:, cols])
        copy = pltpu.make_async_copy(part.at[:, cols], gin_hbm.at[:, cols], out_sem.at[i])
        copy.start()
        outs.append(copy)

    blocks_wait(recv_sem.at[7], crecv, n_dep)
    sums = crecv[...].reshape(64, 128)
    out_in[...] = sums[0:32, 0:64]
    out_out[...] = pltpu.roll(sums, 64, 1)[:, 0:32]
    out_bias[...] = sums[32:33, 0:64]

    for n in range(4):
        eta_sent(n, sends.at[n])
    blocks_wait(send_sem.at[4], arecv, n_dep)
    blocks_wait(send_sem.at[5], drecv, n_dep)
    blocks_wait(send_sem.at[6], brecv, n_eta)
    blocks_wait(send_sem.at[7], crecv, n_dep)
    for copy in outs:
        copy.wait()


def local(n_dep, n_eta, field_in, grad_out, spectral_weight, mlp_in, mlp_bias, mlp_out):
    layers, cells, chans, n_phi = field_in.shape
    owned, n_modes = spectral_weight.shape[1:3]
    n_cells = cells * n_eta
    assert (layers, cells, chans, owned, n_modes) == (2, 4, 32, 2, 64)
    fwd, inv = phi_table(n_phi, owned * n_eta)
    efwd, einv = eta_tables(n_cells, n_modes, n_eta)
    rows = layers * cells * chans
    mb = n_modes // n_dep
    chunk = min(256, n_phi)
    factor = math.sqrt(n_phi * n_cells / (owned * n_eta * n_modes))
    norm = 1.0 / math.sqrt(layers * n_dep * n_cells * n_phi)
    vmem = pl.BlockSpec(memory_space=pltpu.VMEM)
    hbm = pl.BlockSpec(memory_space=pl.ANY)
    part = 64 // n_dep
    scratch = [
        pltpu.VMEM((rows, n_phi), BF16),
        pltpu.VMEM((rows, n_phi), BF16),
        pltpu.VMEM((4 * n_modes, 1024), BF16),
        pltpu.VMEM(fwd.shape, BF16),
        pltpu.VMEM(inv.shape, BF16),
        pltpu.VMEM(efwd.shape, BF16),
        pltpu.VMEM(einv.shape, BF16),
        pltpu.VMEM((2 * rows, n_phi), BF16),
        pltpu.VMEM((2 * rows, n_phi), BF16),
        pltpu.VMEM((rows, n_phi), F32),
        pltpu.VMEM((rows, n_phi), BF16),
        pltpu.VMEM((rows, 4 * n_eta), BF16),
        pltpu.VMEM((256, 128), BF16),
        pltpu.VMEM((128, 256), BF16),
        pltpu.VMEM((128, 256), BF16),
        pltpu.VMEM((256, 128), BF16),
        pltpu.VMEM((256, 128), F32),
        pltpu.VMEM((2, 1024, 128), F32),
        pltpu.VMEM((2, 1024, 128), F32),
        pltpu.VMEM((2, 64, 128), F32),
        pltpu.VMEM((8, 128), F32),
        pltpu.VMEM((4, 8 * n_eta, 128), F32),
        pltpu.VMEM((4, 8 * n_eta, 128), F32),
        pltpu.VMEM((4, 64, 128), F32),
        pltpu.VMEM((n_dep, 4, mb, 128), F32),
        pltpu.VMEM((2, 256, 1024), F32),
        pltpu.VMEM((2, 256, 128), F32),
        pltpu.VMEM((n_dep, part, 128), F32),
        pltpu.VMEM((n_dep, part, 128), F32),
        pltpu.VMEM((part, 128), F32),
        pltpu.VMEM((n_eta, part, 128), F32),
        pltpu.VMEM((part, 128), F32),
        pltpu.VMEM((n_dep, part, 128), F32),
        pltpu.SemaphoreType.DMA((7,)),
        pltpu.SemaphoreType.DMA((n_phi // chunk,)),
        pltpu.SemaphoreType.DMA((8,)),
        pltpu.SemaphoreType.DMA((8,)),
    ]
    gin, gspec, g_in, g_out, g_bias = pl.pallas_call(
        functools.partial(kernel, n_dep, n_eta, chunk, factor, norm),
        out_shape=(
            jax.ShapeDtypeStruct((rows, n_phi), F32),
            jax.ShapeDtypeStruct((2, 2, mb, 1024), F32),
            jax.ShapeDtypeStruct((32, 64), F32),
            jax.ShapeDtypeStruct((64, 32), F32),
            jax.ShapeDtypeStruct((1, 64), F32),
        ),
        in_specs=[hbm, hbm, hbm, vmem, vmem, vmem, hbm, hbm, hbm, hbm],
        out_specs=(hbm, vmem, vmem, vmem, vmem),
        scratch_shapes=scratch,
        compiler_params=pltpu.CompilerParams(
            collective_id=0, has_side_effects=True, vmem_limit_bytes=48 * 1024 * 1024
        ),
    )(
        field_in.reshape(rows, n_phi),
        grad_out.reshape(rows, n_phi),
        spectral_weight.reshape(4 * n_modes, 1024),
        mlp_in,
        mlp_bias.reshape(1, 64),
        mlp_out,
        jnp.asarray(fwd),
        jnp.asarray(inv),
        jnp.asarray(efwd),
        jnp.asarray(einv),
    )
    return gin.reshape(layers, cells, chans, n_phi), gspec, g_in, g_out, g_bias.reshape(64)


def solution(mesh):
    return jax.shard_map(
        functools.partial(local, mesh.shape["depth"], mesh.shape["eta"]),
        mesh=mesh,
        in_specs=(
            P("depth", "eta", None, None),
            P("depth", "eta", None, None),
            P(None, "eta", None, None),
            P(),
            P(),
            P(),
        ),
        out_specs=(P("depth", "eta", None, None), P(None, "eta", "depth", None), P(), P(), P()),
        check_vma=False,
    )
```

```python
import functools
import math

import jax
import jax.numpy as jnp
import ml_dtypes
import numpy as np
from jax import lax
from jax.experimental import pallas as pl
from jax.experimental.pallas import tpu as pltpu
from jax.sharding import PartitionSpec as P

F32 = jnp.float32
BF16 = jnp.bfloat16
MESH = pl.DeviceIdType.MESH


def bf(table):
    return table.astype(np.float32).astype(ml_dtypes.bfloat16)


def phi_table(n_phi, n_modes):
    owners = n_modes // 2
    mode = 2 * np.arange(owners)[None, :] + np.arange(2)[:, None]
    freq = np.where(mode < n_modes // 2, mode, n_phi - n_modes + mode)
    theta = 2.0 * np.pi / n_phi * ((freq[:, :, None] * np.arange(n_phi)) % n_phi)
    pairs = np.stack([np.cos(theta), -np.sin(theta)], axis=1).reshape(4 * owners, n_phi)
    return bf(pairs / math.sqrt(n_phi)), bf(pairs / math.sqrt(n_modes))


def eta_tables(n_eta, n_modes, owners):
    j, hi, lo = np.meshgrid(np.arange(owners), np.arange(2), np.arange(2), indexing="ij")
    cell = 4 * j + 2 * hi + lo
    phase = 2.0 * np.pi / n_eta * ((cell[..., None] * np.arange(n_modes)) % n_eta)
    cosine, sine = np.cos(phase), np.sin(phase)
    fwd = np.zeros((2, owners, 2, 2, 2, 2, 2, n_modes))
    inv = np.zeros((owners, 2, 2, 2, 2, 2, 2, n_modes))
    for low in range(2):
        c, s = cosine[:, :, low], sine[:, :, low]
        for kk in range(2):
            fwd[low, :, kk, 0, :, 0, kk] = c
            fwd[low, :, kk, 1, :, 0, kk] = s
            fwd[low, :, kk, 0, :, 1, kk] = -s
            fwd[low, :, kk, 1, :, 1, kk] = c
            inv[:, kk, 0, :, low, 0, kk] = c
            inv[:, kk, 0, :, low, 1, kk] = -s
            inv[:, kk, 1, :, low, 0, kk] = s
            inv[:, kk, 1, :, low, 1, kk] = c
    fwd = fwd.reshape(2 * 8 * owners, 4 * n_modes) / math.sqrt(n_eta)
    inv = inv.reshape(8 * owners, 8 * n_modes) / math.sqrt(n_modes)
    return bf(fwd), bf(inv)


def far_first(n_eta):
    if n_eta != 32:
        return [(s,) for s in range(1, n_eta)]
    steps = [(x, z, y) for x in range(4) for z in range(2) for y in range(4)]
    return sorted(steps[1:], key=lambda s: -(min(s[0], 4 - s[0]) + s[1] + min(s[2], 4 - s[2])))


def eta_peer(eta, n_eta, step):
    if len(step) == 1:
        return lax.rem(eta + step[0], n_eta)
    x, z, y = eta // 8, lax.rem(eta // 4, 2), lax.rem(eta, 4)
    return lax.rem(x + step[0], 4) * 8 + lax.rem(z + step[1], 2) * 4 + lax.rem(y + step[2], 4)


def nn(a, b):
    return lax.dot_general(a, b, (((1,), (0,)), ((), ())), preferred_element_type=F32)


def nt(a, b):
    return lax.dot_general(a, b, (((1,), (1,)), ((), ())), preferred_element_type=F32)


def cdf_and_density(v):
    cdf = 0.5 + 0.5 * lax.erf(v * (1.0 / math.sqrt(2.0)))
    density = jnp.exp(-0.5 * v * v) * (1.0 / math.sqrt(2.0 * math.pi))
    return cdf, density


def eta_order(x):
    blocks = [x[b * 32 : (b + 1) * 32] for b in range(8)]
    return jnp.concatenate([blocks[d * 4 + hi * 2 + lo] for hi in range(2) for lo in range(2) for d in range(2)], axis=0)


def cell_order(x):
    blocks = [x[b * 32 : (b + 1) * 32] for b in range(8)]
    return jnp.concatenate([blocks[hi * 4 + lo * 2 + d] for d in range(2) for hi in range(2) for lo in range(2)], axis=0)


def kernel(
    n_dep,
    n_eta,
    chunk,
    factor,
    norm,
    field_hbm,
    cotan_hbm,
    weight_hbm,
    mlp_in_hbm,
    mlp_bias_hbm,
    mlp_outt_hbm,
    fwd_hbm,
    inv_hbm,
    efwd_hbm,
    einv_hbm,
    part,
    gspec,
    out_in,
    out_out,
    out_bias,
    field,
    cotan,
    weight,
    tfwd,
    tinv,
    efwd,
    einv,
    hid,
    slope,
    gpre,
    w_all,
    m_up,
    m_down,
    m_outt,
    m_out,
    bias_col,
    rt,
    rt2,
    zbuf,
    mlp_in,
    mlp_bias,
    mlp_outt,
    sends,
    recvs,
    dsend,
    drecv,
    xexp,
    gexp,
    asend,
    arecv,
    bsend,
    brecv,
    csend,
    crecv,
    load_sem,
    send_sem,
    recv_sem,
):
    dep = lax.axis_index("depth")
    eta = lax.axis_index("eta")
    n_phi = field.shape[1]
    n_chunks = n_phi // chunk

    barrier = pltpu.get_barrier_semaphore()

    eta_peers = [eta_peer(eta, n_eta, step) for step in far_first(n_eta)]
    dep_peers = [lax.rem(dep + s, n_dep) for s in range(1, n_dep)]
    for peer in eta_peers:
        pl.semaphore_signal(barrier, inc=1, device_id=(dep, peer), device_id_type=MESH)
    for peer in dep_peers:
        pl.semaphore_signal(barrier, inc=1, device_id=(peer, eta), device_id_type=MESH)

    loads = [
        pltpu.make_async_copy(src, dst, load_sem.at[n])
        for n, (src, dst) in enumerate(
            (
                (field_hbm, field),
                (fwd_hbm, tfwd),
                (efwd_hbm, efwd),
                (einv_hbm, einv),
                (weight_hbm, weight),
                (inv_hbm, tinv),
                (cotan_hbm, cotan),
                (mlp_in_hbm, mlp_in),
                (mlp_bias_hbm, mlp_bias),
                (mlp_outt_hbm, mlp_outt),
            )
        )
    ]
    for copy in loads:
        copy.start()

    def eta_start(n, send, recv):
        for peer in eta_peers:
            pltpu.make_async_remote_copy(
                src_ref=send.at[pl.ds(pl.multiple_of(peer * 8, 8), 8)],
                dst_ref=recv.at[pl.ds(pl.multiple_of(eta * 8, 8), 8)],
                send_sem=send_sem.at[n],
                recv_sem=recv_sem.at[n],
                device_id=(dep, peer),
                device_id_type=MESH,
            ).start()
        own = pl.ds(pl.multiple_of(eta * 8, 8), 8)
        recv[own, :] = send[own, :]

    def eta_wait(n, recv):
        rows = pl.ds(0, 8 * (n_eta - 1))
        pltpu.make_async_copy(recv.at[rows], recv.at[rows], recv_sem.at[n]).wait()

    def eta_sent(n, send):
        rows = pl.ds(0, 8 * (n_eta - 1))
        pltpu.make_async_copy(send.at[rows], send.at[rows], send_sem.at[n]).wait()

    def gather_start(n, axis, block, recv):
        me, peers = (dep, dep_peers) if axis == "depth" else (eta, eta_peers)
        for peer in peers:
            pltpu.make_async_remote_copy(
                src_ref=block,
                dst_ref=recv.at[me],
                send_sem=send_sem.at[n],
                recv_sem=recv_sem.at[n],
                device_id=(peer, eta) if axis == "depth" else (dep, peer),
                device_id_type=MESH,
            ).start()
        recv[me] = block[...]

    def blocks_wait(sem, recv, count):
        some = pl.ds(0, count - 1)
        pltpu.make_async_copy(recv.at[some], recv.at[some], sem).wait()

    def phi_forward(x, send):
        spectra = nt(tfwd[...], eta_order(x))
        for q in range(4):
            for hi in range(2):
                send[pl.ds(q * 2 + hi, n_eta, stride=8), :] = spectra[
                    q * n_eta : (q + 1) * n_eta, hi * 128 : (hi + 1) * 128
                ]

    def eta_forward(recv):
        xt = recv[...].T.astype(BF16)
        half = 8 * n_eta
        return nn(xt[0:64], efwd[0:half, :]) + nn(xt[64:128], efwd[half:, :])

    def eta_inverse(real, imag, send):
        v = jnp.concatenate([real, imag], axis=1).astype(BF16)
        zero = jnp.zeros_like(v)
        both = jnp.concatenate(
            [jnp.concatenate([v, zero], axis=1), jnp.concatenate([zero, v], axis=1)], axis=0
        )
        send[...] = nt(einv[...], both)

    def phi_inverse_lhs(recv):
        halves = []
        for hi in range(2):
            rows = [recv[pl.ds(q * 2 + hi, n_eta, stride=8), :] for q in range(4)]
            halves.append(jnp.concatenate(rows, axis=0).T)
        w_all[...] = cell_order(jnp.concatenate(halves, axis=0)).astype(BF16)

    loads[0].wait()
    loads[1].wait()
    phi_forward(field[...], sends.at[0])
    pl.semaphore_wait(barrier, n_eta + n_dep - 2)
    eta_start(0, sends.at[0], recvs.at[0])

    for copy in loads[7:]:
        copy.wait()

    def tile_rows(x):
        return jnp.concatenate([x] * 4, axis=0)

    spread = (
        lax.broadcasted_iota(jnp.int32, (64, 256), 0) == lax.rem(lax.broadcasted_iota(jnp.int32, (64, 256), 1), 64)
    ).astype(F32).astype(BF16)
    keep = (
        lax.broadcasted_iota(jnp.int32, (128, 256), 0) // 32 == lax.broadcasted_iota(jnp.int32, (128, 256), 1) // 64
    )
    for matrix, wide, tall in ((mlp_in, m_down, m_up), (mlp_outt, m_outt, m_out)):
        four = jnp.where(keep, tile_rows(nn(matrix[...], spread)), 0.0)
        wide[...] = four.astype(BF16)
        tall[...] = four.T.astype(BF16)
    diagonal = lax.broadcasted_iota(jnp.int32, (64, 64), 0) == lax.broadcasted_iota(jnp.int32, (64, 64), 1)
    column = jnp.sum(jnp.where(diagonal, mlp_bias[...], 0.0), axis=1, keepdims=True)
    bias_col[...] = jnp.broadcast_to(tile_rows(column), (256, 128))

    def mlp_forward(g):
        def body(i, c):
            cols = pl.ds(pl.multiple_of(i * chunk, chunk), chunk)
            pre = nn(m_up[...], field[g * 128 : (g + 1) * 128, cols])
            pre = pre + jnp.concatenate([bias_col[...]] * (chunk // 128), axis=1)
            cdf, density = cdf_and_density(pre)
            hidden = (pre * cdf).astype(BF16)
            hid[g * 256 : (g + 1) * 256, cols] = hidden
            slope[g * 256 : (g + 1) * 256, cols] = (cdf + pre * density).astype(BF16)
            part[g * 128 : (g + 1) * 128, cols] = nn(m_outt[...], hidden)
            return c

        lax.fori_loop(0, n_chunks, body, 0)

    loads[4].wait()
    for ri in range(2):
        rt[ri] = weight[ri * 128 : (ri + 1) * 128, :].astype(F32).T
    mlp_forward(0)

    loads[2].wait()
    loads[3].wait()
    eta_wait(0, recvs.at[0])
    zx = eta_forward(recvs.at[0])
    for ri in range(2):
        zbuf[ri] = zx[:, ri * 128 : (ri + 1) * 128]
    dsend_x = zx

    def mix(table, sign):
        real = [jnp.zeros((32, 128), F32) for _ in range(2)]
        imag = [jnp.zeros((32, 128), F32) for _ in range(2)]
        for c in range(32):
            wr = table[0, c * 32 : (c + 1) * 32, :]
            wi = table[1, c * 32 : (c + 1) * 32, :]
            for d in range(2):
                zr = zbuf[0, d * 32 + c : d * 32 + c + 1, :]
                zi = zbuf[1, d * 32 + c : d * 32 + c + 1, :]
                real[d] = real[d] + (zr * wr - sign * (zi * wi))
                imag[d] = imag[d] + (zi * wr + sign * (zr * wi))
        return jnp.concatenate(real, axis=0), jnp.concatenate(imag, axis=0)

    vr, vi = mix(rt, 1.0)
    eta_inverse(vr, vi, sends.at[1])
    eta_start(1, sends.at[1], recvs.at[1])

    dsend[:, :, 0:64] = dsend_x.T.reshape(4, 64, 64)
    mlp_forward(1)
    for ri in range(2):
        for o in range(32):
            rt2[ri, o * 32 : (o + 1) * 32, :] = rt[ri, pl.ds(o, 32, stride=32), :]

    loads[5].wait()
    loads[6].wait()
    eta_wait(1, recvs.at[1])
    phi_inverse_lhs(recvs.at[1])

    def pre_body(i, c):
        cols = pl.ds(pl.multiple_of(i * chunk, chunk), chunk)
        pre = nn(w_all[...], tinv[:, cols]) + part[:, cols]
        cdf, density = cdf_and_density(pre)
        gpre[:, cols] = (cotan[:, cols].astype(F32) * (cdf + pre * density)).astype(BF16)
        return c

    lax.fori_loop(0, n_chunks, pre_body, 0)
    phi_forward(gpre[...], sends.at[2])
    eta_start(2, sends.at[2], recvs.at[2])

    def mlp_backward(g):
        def body(i, c):
            cols = pl.ds(pl.multiple_of(i * chunk, chunk), chunk)
            grad = nn(m_out[...], gpre[g * 128 : (g + 1) * 128, cols])
            slope[g * 256 : (g + 1) * 256, cols] = (
                grad * slope[g * 256 : (g + 1) * 256, cols].astype(F32)
            ).astype(BF16)
            return c

        lax.fori_loop(0, n_chunks, body, 0)

    def mlp_to_input(g):
        def body(i, c):
            cols = pl.ds(pl.multiple_of(i * chunk, chunk), chunk)
            rows = slice(g * 128, (g + 1) * 128)
            part[rows, cols] = cotan[rows, cols].astype(F32) + nn(
                m_down[...], slope[g * 256 : (g + 1) * 256, cols]
            )
            return c

        lax.fori_loop(0, n_chunks, body, 0)

    def fold(x):
        rows = x.shape[0] // 4 if x.shape[0] > 8 else 0
        acc = None
        for a in range(4):
            tile = x[a * rows : a * rows + (rows or 8), (a // 2) * 128 : (a // 2 + 1) * 128]
            tile = pltpu.roll(tile, 64, 1) if a % 2 else tile
            acc = tile if acc is None else acc + tile
        return acc

    sum_in = jnp.zeros((32, 128), F32)
    sum_out = jnp.zeros((32, 128), F32)
    sum_bias = jnp.zeros((8, 128), F32)
    ones = jnp.ones((8, n_phi), BF16)
    for g in range(2):
        mlp_backward(g)
        grads = slope[g * 256 : (g + 1) * 256, :]
        sum_in = sum_in + fold(nt(field[g * 128 : (g + 1) * 128, :], grads))
        sum_out = sum_out + fold(nt(gpre[g * 128 : (g + 1) * 128, :], hid[g * 256 : (g + 1) * 256, :]))
        sum_bias = sum_bias + fold(nt(ones, grads))
    lane32 = lax.broadcasted_iota(jnp.int32, (32, 128), 1)
    total = jnp.concatenate(
        [jnp.where(lane32 < 64, sum_in, pltpu.roll(sum_out, 64, 1)), sum_bias, jnp.zeros((24, 128), F32)],
        axis=0,
    )
    asend[...] = total.reshape(asend.shape)

    for peer in dep_peers:
        pltpu.make_async_remote_copy(
            src_ref=asend.at[peer],
            dst_ref=arecv.at[dep],
            send_sem=send_sem.at[4],
            recv_sem=recv_sem.at[4],
            device_id=(peer, eta),
            device_id_type=MESH,
        ).start()
    arecv[dep] = asend[dep]

    eta_wait(2, recvs.at[2])
    zg = eta_forward(recvs.at[2])
    for ri in range(2):
        zbuf[ri] = zg[:, ri * 128 : (ri + 1) * 128]
    br, bi = mix(rt2, -1.0)
    eta_inverse(br, bi, sends.at[3])
    eta_start(3, sends.at[3], recvs.at[3])

    dsend[:, :, 64:128] = zg.T.reshape(4, 64, 64)
    mb = drecv.shape[2]

    for peer in dep_peers:
        pltpu.make_async_remote_copy(
            src_ref=dsend.at[:, pl.ds(pl.multiple_of(peer * mb, mb), mb), :],
            dst_ref=drecv.at[dep],
            send_sem=send_sem.at[5],
            recv_sem=recv_sem.at[5],
            device_id=(peer, eta),
            device_id_type=MESH,
        ).start()
    drecv[dep] = dsend[:, pl.ds(pl.multiple_of(dep * mb, mb), mb), :]

    mlp_to_input(0)
    blocks_wait(recv_sem.at[4], arecv, n_dep)
    mine = arecv[0]
    for i in range(1, n_dep):
        mine = mine + arecv[i]
    bsend[...] = mine
    gather_start(6, "eta", bsend, brecv)

    mlp_to_input(1)

    blocks_wait(recv_sem.at[5], drecv, n_dep)
    got = drecv[...].reshape(256, 128)
    lane = lax.broadcasted_iota(jnp.int32, (256, 128), 1)
    row_c = lax.rem(lax.broadcasted_iota(jnp.int32, (128, 1024), 0), 32)
    repeat = (row_c == lax.broadcasted_iota(jnp.int32, (128, 1024), 1) // 32).astype(F32).astype(BF16)
    row_o = lax.rem(lax.broadcasted_iota(jnp.int32, (128, 128), 0), 32)
    tiled = (row_o == lax.rem(lax.broadcasted_iota(jnp.int32, (128, 128), 1), 32)).astype(F32).astype(BF16)
    for d in range(2):
        xexp[d] = nn(jnp.where(lane // 32 == d, got, 0.0).astype(BF16), repeat)
        gexp[d] = nn(jnp.where(lane // 32 == 2 + d, got, 0.0).astype(BF16), tiled)
    for kk in range(2):
        for t in range(8):
            lanes = slice(t * 128, (t + 1) * 128)
            real = jnp.zeros((mb, 128), F32)
            imag = jnp.zeros((mb, 128), F32)
            for i in range(n_dep):
                r0 = (i * 4 + kk) * mb
                r1 = (i * 4 + 2 + kk) * mb
                for d in range(2):
                    xr = xexp[d, r0 : r0 + mb, lanes]
                    xi = xexp[d, r1 : r1 + mb, lanes]
                    gr = gexp[d, r0 : r0 + mb, :]
                    gi = gexp[d, r1 : r1 + mb, :]
                    real = real + (xr * gr + xi * gi)
                    imag = imag + (xr * gi - xi * gr)
            gspec[0, kk, :, lanes] = real * factor
            gspec[1, kk, :, lanes] = imag * factor

    eta_wait(3, recvs.at[3])
    phi_inverse_lhs(recvs.at[3])

    def gin_body(i, c):
        cols = pl.ds(pl.multiple_of(i * chunk, chunk), chunk)
        part[:, cols] = part[:, cols] + nn(w_all[...], tinv[:, cols])
        return c

    lax.fori_loop(0, n_chunks, gin_body, 0)

    blocks_wait(recv_sem.at[6], brecv, n_eta)
    mine = brecv[0]
    for i in range(1, n_eta):
        mine = mine + brecv[i]
    csend[...] = mine * norm
    gather_start(7, "depth", csend, crecv)
    blocks_wait(recv_sem.at[7], crecv, n_dep)
    sums = crecv[...].reshape(64, 128)
    out_in[...] = sums[0:32, 0:64]
    out_out[...] = pltpu.roll(sums[0:32, :], 64, 1)[:, 0:64]
    out_bias[...] = sums[32:33, 0:64]

    for n in range(4):
        eta_sent(n, sends.at[n])
    blocks_wait(send_sem.at[4], arecv, n_dep)
    blocks_wait(send_sem.at[5], drecv, n_dep)
    blocks_wait(send_sem.at[6], brecv, n_eta)
    blocks_wait(send_sem.at[7], crecv, n_dep)


def write_out(*refs):
    ins, outs, sem = refs[:5], refs[5:10], refs[10]
    copies = [pltpu.make_async_copy(src, dst, sem.at[n]) for n, (src, dst) in enumerate(zip(ins, outs))]
    for copy in copies:
        copy.start()
    for copy in copies:
        copy.wait()


def local(n_dep, n_eta, field_in, grad_out, spectral_weight, mlp_in, mlp_bias, mlp_out):
    layers, cells, chans, n_phi = field_in.shape
    owned, n_modes = spectral_weight.shape[1:3]
    n_cells = cells * n_eta
    assert (layers, cells, chans, owned, n_modes) == (2, 4, 32, 2, 64)
    fwd, inv = phi_table(n_phi, owned * n_eta)
    efwd, einv = eta_tables(n_cells, n_modes, n_eta)
    rows = layers * cells * chans
    mb = n_modes // n_dep
    chunk = min(256, n_phi)
    factor = math.sqrt(n_phi * n_cells / (owned * n_eta * n_modes))
    norm = 1.0 / math.sqrt(layers * n_dep * n_cells * n_phi)
    vmem = pl.BlockSpec(memory_space=pltpu.VMEM)
    hbm = pl.BlockSpec(memory_space=pltpu.HBM)
    part = 64 // n_dep
    scratch = [
        pltpu.VMEM((rows, n_phi), BF16),
        pltpu.VMEM((rows, n_phi), BF16),
        pltpu.VMEM((4 * n_modes, 1024), BF16),
        pltpu.VMEM(fwd.shape, BF16),
        pltpu.VMEM(inv.shape, BF16),
        pltpu.VMEM(efwd.shape, BF16),
        pltpu.VMEM(einv.shape, BF16),
        pltpu.VMEM((2 * rows, n_phi), BF16),
        pltpu.VMEM((2 * rows, n_phi), BF16),
        pltpu.VMEM((rows, n_phi), BF16),
        pltpu.VMEM((rows, 4 * n_eta), BF16),
        pltpu.VMEM((256, 128), BF16),
        pltpu.VMEM((128, 256), BF16),
        pltpu.VMEM((128, 256), BF16),
        pltpu.VMEM((256, 128), BF16),
        pltpu.VMEM((256, 128), F32),
        pltpu.VMEM((2, 1024, 128), F32),
        pltpu.VMEM((2, 1024, 128), F32),
        pltpu.VMEM((2, 64, 128), F32),
        pltpu.VMEM((32, 64), BF16),
        pltpu.VMEM((1, 64), F32),
        pltpu.VMEM((32, 64), BF16),
        pltpu.VMEM((4, 8 * n_eta, 128), F32),
        pltpu.VMEM((4, 8 * n_eta, 128), F32),
        pltpu.VMEM((4, 64, 128), F32),
        pltpu.VMEM((n_dep, 4, mb, 128), F32),
        pltpu.VMEM((2, 256, 1024), F32),
        pltpu.VMEM((2, 256, 128), F32),
        pltpu.VMEM((n_dep, part, 128), F32),
        pltpu.VMEM((n_dep, part, 128), F32),
        pltpu.VMEM((part, 128), F32),
        pltpu.VMEM((n_eta, part, 128), F32),
        pltpu.VMEM((part, 128), F32),
        pltpu.VMEM((n_dep, part, 128), F32),
        pltpu.SemaphoreType.DMA((10,)),
        pltpu.SemaphoreType.DMA((8,)),
        pltpu.SemaphoreType.DMA((8,)),
    ]
    sizes = ((rows, n_phi), (2, 2, mb, 1024), (32, 64), (32, 64), (1, 64))
    operands = (
        field_in.reshape(rows, n_phi),
        grad_out.reshape(rows, n_phi),
        spectral_weight.reshape(4 * n_modes, 1024),
        mlp_in,
        mlp_bias.reshape(1, 64),
        mlp_out.T,
        jnp.asarray(fwd),
        jnp.asarray(inv),
        jnp.asarray(efwd),
        jnp.asarray(einv),
    )
    results = pl.pallas_call(
        functools.partial(kernel, n_dep, n_eta, chunk, factor, norm),
        out_shape=tuple(pltpu.VMEM(size, F32) for size in sizes),
        in_specs=[hbm] * 10,
        out_specs=(vmem,) * 5,
        scratch_shapes=scratch,
        compiler_params=pltpu.CompilerParams(
            collective_id=0, has_side_effects=True, vmem_limit_bytes=48 * 1024 * 1024
        ),
    )(*(pltpu.with_memory_space_constraint(x, pltpu.HBM) for x in operands))
    gin, gspec, g_in, g_outt, g_bias = pl.pallas_call(
        write_out,
        out_shape=tuple(jax.ShapeDtypeStruct(size, F32) for size in sizes),
        in_specs=[vmem] * 5,
        out_specs=(hbm,) * 5,
        scratch_shapes=[pltpu.SemaphoreType.DMA((5,))],
    )(*(pltpu.with_memory_space_constraint(x, pltpu.VMEM) for x in results))
    return gin.reshape(layers, cells, chans, n_phi), gspec, g_in, g_outt.T, g_bias.reshape(64)


def solution(mesh):
    return jax.shard_map(
        functools.partial(local, mesh.shape["depth"], mesh.shape["eta"]),
        mesh=mesh,
        in_specs=(
            P("depth", "eta", None, None),
            P("depth", "eta", None, None),
            P(None, "eta", None, None),
            P(),
            P(),
            P(),
        ),
        out_specs=(P("depth", "eta", None, None), P(None, "eta", "depth", None), P(), P(), P()),
        check_vma=False,
    )
```

```python
import functools
import math

import jax
import jax.numpy as jnp
import ml_dtypes
import numpy as np
from jax import lax
from jax.experimental import pallas as pl
from jax.experimental.pallas import tpu as pltpu
from jax.sharding import PartitionSpec as P

F32 = jnp.float32
BF16 = jnp.bfloat16
MESH = pl.DeviceIdType.MESH
CHUNK = 2048
OUT_CHUNK = 512


def bf(table):
    return table.astype(np.float32).astype(ml_dtypes.bfloat16)


def phi_table(n_phi, n_modes):
    owners = n_modes // 2
    mode = 2 * np.arange(owners)[None, :] + np.arange(2)[:, None]
    freq = np.where(mode < n_modes // 2, mode, n_phi - n_modes + mode)
    theta = 2.0 * np.pi / n_phi * ((freq[:, :, None] * np.arange(n_phi)) % n_phi)
    pairs = np.stack([np.cos(theta), -np.sin(theta)], axis=1).reshape(4 * owners, n_phi)
    return bf(pairs / math.sqrt(n_phi)), bf(pairs / math.sqrt(n_modes))


def eta_tables(n_eta, n_modes, owners):
    j, hi, lo = np.meshgrid(np.arange(owners), np.arange(2), np.arange(2), indexing="ij")
    cell = 4 * j + 2 * hi + lo
    phase = 2.0 * np.pi / n_eta * ((cell[..., None] * np.arange(n_modes)) % n_eta)
    cosine, sine = np.cos(phase), np.sin(phase)
    fwd = np.zeros((2, owners, 2, 2, 2, 2, 2, n_modes))
    inv = np.zeros((owners, 2, 2, 2, 2, 2, 2, n_modes))
    for low in range(2):
        c, s = cosine[:, :, low], sine[:, :, low]
        for kk in range(2):
            fwd[low, :, kk, 0, :, 0, kk] = c
            fwd[low, :, kk, 1, :, 0, kk] = s
            fwd[low, :, kk, 0, :, 1, kk] = -s
            fwd[low, :, kk, 1, :, 1, kk] = c
            inv[:, kk, 0, :, low, 0, kk] = c
            inv[:, kk, 0, :, low, 1, kk] = -s
            inv[:, kk, 1, :, low, 0, kk] = s
            inv[:, kk, 1, :, low, 1, kk] = c
    fwd = fwd.reshape(2 * 8 * owners, 4 * n_modes) / math.sqrt(n_eta)
    inv = inv.reshape(8 * owners, 8 * n_modes) / math.sqrt(n_modes)
    return bf(fwd), bf(inv)


def far_first(n_eta):
    if n_eta != 32:
        return [(s,) for s in range(1, n_eta)]
    steps = [(x, z, y) for x in range(4) for z in range(2) for y in range(4)]
    return sorted(steps[1:], key=lambda s: -(min(s[0], 4 - s[0]) + s[1] + min(s[2], 4 - s[2])))


def eta_peer(eta, n_eta, step):
    if len(step) == 1:
        return lax.rem(eta + step[0], n_eta)
    x, z, y = eta // 8, lax.rem(eta // 4, 2), lax.rem(eta, 4)
    return lax.rem(x + step[0], 4) * 8 + lax.rem(z + step[1], 2) * 4 + lax.rem(y + step[2], 4)


def nn(a, b):
    return lax.dot_general(a, b, (((1,), (0,)), ((), ())), preferred_element_type=F32)


def nt(a, b):
    return lax.dot_general(a, b, (((1,), (1,)), ((), ())), preferred_element_type=F32)


def cdf_and_density(v):
    cdf = 0.5 + 0.5 * lax.erf(v * (1.0 / math.sqrt(2.0)))
    density = jnp.exp(-0.5 * v * v) * (1.0 / math.sqrt(2.0 * math.pi))
    return cdf, density


ONES = 16


def field_rows(d):
    return slice(d * (128 + ONES), d * (128 + ONES) + 128)


def eta_order(x, gap=0):
    blocks = [x[b * 32 + b // 4 * gap : (b + 1) * 32 + b // 4 * gap] for b in range(8)]
    return jnp.concatenate([blocks[d * 4 + hi * 2 + lo] for hi in range(2) for lo in range(2) for d in range(2)], axis=0)


def cell_order(x):
    blocks = [x[b * 32 : (b + 1) * 32] for b in range(8)]
    return jnp.concatenate([blocks[hi * 4 + lo * 2 + d] for d in range(2) for hi in range(2) for lo in range(2)], axis=0)


def kernel(
    n_dep,
    n_eta,
    chunk,
    factor,
    norm,
    field_hbm,
    cotan_hbm,
    weight_hbm,
    mlp_in_hbm,
    mlp_bias_hbm,
    mlp_outt_hbm,
    fwd_hbm,
    inv_hbm,
    efwd_hbm,
    einv_hbm,
    part,
    w_all,
    tinv,
    gspec,
    out_in,
    out_out,
    out_bias,
    field,
    cotan,
    weight,
    tfwd,
    efwd,
    einv,
    hid,
    slope,
    gpre,
    m_up,
    m_down,
    m_outt,
    m_out,
    bias_col,
    rt,
    rt2,
    zbuf,
    mlp_in,
    mlp_bias,
    mlp_outt,
    sends,
    recvs,
    dsend,
    drecv,
    xexp,
    gexp,
    asend,
    arecv,
    bsend,
    brecv,
    absend,
    abrecv,
    bbsend,
    bbrecv,
    load_sem,
    send_sem,
    recv_sem,
):
    dep = lax.axis_index("depth")
    eta = lax.axis_index("eta")
    n_phi = field.shape[1]
    n_chunks = n_phi // chunk

    barrier = pltpu.get_barrier_semaphore()

    eta_peers = [eta_peer(eta, n_eta, step) for step in far_first(n_eta)]
    dep_peers = [lax.rem(dep + s, n_dep) for s in range(1, n_dep)]
    for peer in eta_peers:
        pl.semaphore_signal(barrier, inc=1, device_id=(dep, peer), device_id_type=MESH)
    for peer in dep_peers:
        pl.semaphore_signal(barrier, inc=1, device_id=(peer, eta), device_id_type=MESH)

    loads = [
        pltpu.make_async_copy(src, dst, load_sem.at[n])
        for n, (src, dst) in enumerate(
            (
                (field_hbm.at[pl.ds(0, 128)], field.at[pl.ds(0, 128)]),
                (field_hbm.at[pl.ds(128, 128)], field.at[pl.ds(128 + ONES, 128)]),
                (fwd_hbm, tfwd),
                (efwd_hbm, efwd),
                (einv_hbm, einv),
                (weight_hbm, weight),
                (inv_hbm, tinv),
                (cotan_hbm, cotan),
                (mlp_in_hbm, mlp_in),
                (mlp_bias_hbm, mlp_bias),
                (mlp_outt_hbm, mlp_outt),
            )
        )
    ]
    for copy in loads:
        copy.start()
    field[128 : 128 + ONES, :] = jnp.ones((ONES, n_phi), BF16)

    def eta_start(n, send, recv):
        for peer in eta_peers:
            pltpu.make_async_remote_copy(
                src_ref=send.at[pl.ds(pl.multiple_of(peer * 8, 8), 8)],
                dst_ref=recv.at[pl.ds(pl.multiple_of(eta * 8, 8), 8)],
                send_sem=send_sem.at[n],
                recv_sem=recv_sem.at[n],
                device_id=(dep, peer),
                device_id_type=MESH,
            ).start()
        own = pl.ds(pl.multiple_of(eta * 8, 8), 8)
        recv[own, :] = send[own, :]

    def eta_wait(n, recv):
        rows = pl.ds(0, 8 * (n_eta - 1))
        pltpu.make_async_copy(recv.at[rows], recv.at[rows], recv_sem.at[n]).wait()

    def eta_sent(n, send):
        rows = pl.ds(0, 8 * (n_eta - 1))
        pltpu.make_async_copy(send.at[rows], send.at[rows], send_sem.at[n]).wait()

    def gather_start(n, axis, block, recv):
        me, peers = (dep, dep_peers) if axis == "depth" else (eta, eta_peers)
        for peer in peers:
            pltpu.make_async_remote_copy(
                src_ref=block,
                dst_ref=recv.at[me],
                send_sem=send_sem.at[n],
                recv_sem=recv_sem.at[n],
                device_id=(peer, eta) if axis == "depth" else (dep, peer),
                device_id_type=MESH,
            ).start()
        recv[me] = block[...]

    def blocks_wait(sem, recv, count):
        some = pl.ds(0, count - 1)
        pltpu.make_async_copy(recv.at[some], recv.at[some], sem).wait()

    def phi_forward(x, send, gap=0):
        spectra = nt(tfwd[...], eta_order(x, gap))
        for q in range(4):
            for hi in range(2):
                send[pl.ds(q * 2 + hi, n_eta, stride=8), :] = spectra[
                    q * n_eta : (q + 1) * n_eta, hi * 128 : (hi + 1) * 128
                ]

    def eta_forward(recv):
        xt = recv[...].T.astype(BF16)
        half = 8 * n_eta
        return nn(xt[0:64], efwd[0:half, :]) + nn(xt[64:128], efwd[half:, :])

    def eta_inverse(real, imag, send):
        v = jnp.concatenate([real, imag], axis=1).astype(BF16)
        zero = jnp.zeros_like(v)
        both = jnp.concatenate(
            [jnp.concatenate([v, zero], axis=1), jnp.concatenate([zero, v], axis=1)], axis=0
        )
        send[...] = nt(einv[...], both)

    def phi_inverse_lhs(recv):
        halves = []
        for hi in range(2):
            rows = [recv[pl.ds(q * 2 + hi, n_eta, stride=8), :] for q in range(4)]
            halves.append(jnp.concatenate(rows, axis=0).T)
        w_all[...] = cell_order(jnp.concatenate(halves, axis=0)).astype(BF16)

    for copy in loads[:3]:
        copy.wait()
    phi_forward(field[...], sends.at[0], ONES)
    pl.semaphore_wait(barrier, n_eta + n_dep - 2)
    eta_start(0, sends.at[0], recvs.at[0])

    for copy in loads[8:]:
        copy.wait()

    def tile_rows(x):
        return jnp.concatenate([x] * 4, axis=0)

    spread = (
        lax.broadcasted_iota(jnp.int32, (64, 256), 0) == lax.rem(lax.broadcasted_iota(jnp.int32, (64, 256), 1), 64)
    ).astype(F32).astype(BF16)
    keep = (
        lax.broadcasted_iota(jnp.int32, (128, 256), 0) // 32 == lax.broadcasted_iota(jnp.int32, (128, 256), 1) // 64
    )
    for matrix, wide, tall in ((mlp_in, m_down, m_up), (mlp_outt, m_outt, m_out)):
        four = jnp.where(keep, tile_rows(nn(matrix[...], spread)), 0.0)
        wide[...] = four.astype(BF16)
        tall[...] = four.T.astype(BF16)
    diagonal = lax.broadcasted_iota(jnp.int32, (64, 64), 0) == lax.broadcasted_iota(jnp.int32, (64, 64), 1)
    column = jnp.sum(jnp.where(diagonal, mlp_bias[...], 0.0), axis=1, keepdims=True)
    bias_col[...] = jnp.broadcast_to(tile_rows(column), (256, 128))

    def mlp_forward(g):
        def body(i):
            cols = pl.ds(i * chunk, chunk)
            pre = nn(m_up[...], field[field_rows(g), cols])
            pre = pre + jnp.concatenate([bias_col[...]] * (chunk // 128), axis=1)
            cdf, density = cdf_and_density(pre)
            hidden = (pre * cdf).astype(BF16)
            hid[g * 256 : (g + 1) * 256, cols] = hidden
            slope[g * 256 : (g + 1) * 256, cols] = (cdf + pre * density).astype(BF16)
            part[g * 128 : (g + 1) * 128, cols] = nn(m_outt[...], hidden)

        for i in range(n_chunks):
            body(i)

    loads[5].wait()
    for ri in range(2):
        rt[ri] = weight[ri * 128 : (ri + 1) * 128, :].astype(F32).T
    mlp_forward(0)

    loads[3].wait()
    loads[4].wait()
    eta_wait(0, recvs.at[0])
    zx = eta_forward(recvs.at[0])
    for ri in range(2):
        zbuf[ri] = zx[:, ri * 128 : (ri + 1) * 128]
    dsend_x = zx

    def mix(table, sign):
        real = [jnp.zeros((32, 128), F32) for _ in range(2)]
        imag = [jnp.zeros((32, 128), F32) for _ in range(2)]
        for c in range(32):
            wr = table[0, c * 32 : (c + 1) * 32, :]
            wi = table[1, c * 32 : (c + 1) * 32, :]
            for d in range(2):
                zr = zbuf[0, d * 32 + c : d * 32 + c + 1, :]
                zi = zbuf[1, d * 32 + c : d * 32 + c + 1, :]
                real[d] = real[d] + (zr * wr - sign * (zi * wi))
                imag[d] = imag[d] + (zi * wr + sign * (zr * wi))
        return jnp.concatenate(real, axis=0), jnp.concatenate(imag, axis=0)

    vr, vi = mix(rt, 1.0)
    eta_inverse(vr, vi, sends.at[1])
    eta_start(1, sends.at[1], recvs.at[1])

    dsend[:, :, 0:64] = dsend_x.T.reshape(4, 64, 64)
    mlp_forward(1)
    for ri in range(2):
        for o in range(32):
            rt2[ri, o * 32 : (o + 1) * 32, :] = rt[ri, pl.ds(o, 32, stride=32), :]

    loads[6].wait()
    loads[7].wait()
    eta_wait(1, recvs.at[1])
    phi_inverse_lhs(recvs.at[1])

    def pre_chunk(i):
        cols = pl.ds(i * chunk, chunk)
        pre = nn(w_all[...], tinv[:, cols]) + part[:, cols]
        cdf, density = cdf_and_density(pre)
        grad = (cotan[:, cols].astype(F32) * (cdf + pre * density)).astype(BF16)
        gpre[:, cols] = grad

    for i in range(n_chunks):
        pre_chunk(i)
    phi_forward(gpre[...], sends.at[2])
    eta_start(2, sends.at[2], recvs.at[2])

    def mlp_backward(g):
        def body(i):
            cols = pl.ds(i * chunk, chunk)
            grad = nn(m_out[...], gpre[g * 128 : (g + 1) * 128, cols])
            slope[g * 256 : (g + 1) * 256, cols] = (
                grad * slope[g * 256 : (g + 1) * 256, cols].astype(F32)
            ).astype(BF16)

        for i in range(n_chunks):
            body(i)

    def mlp_to_input(g):
        def body(i):
            cols = pl.ds(i * chunk, chunk)
            rows = slice(g * 128, (g + 1) * 128)
            part[rows, cols] = cotan[rows, cols].astype(F32) + nn(
                m_down[...], slope[g * 256 : (g + 1) * 256, cols]
            )

        for i in range(n_chunks):
            body(i)

    def fold(x):
        rows = x.shape[0] // 4 if x.shape[0] > 8 else 0
        acc = None
        for a in range(4):
            tile = x[a * rows : a * rows + (rows or 8), (a // 2) * 128 : (a // 2 + 1) * 128]
            tile = pltpu.roll(tile, 64, 1) if a % 2 else tile
            acc = tile if acc is None else acc + tile
        return acc

    sum_in = jnp.zeros((32, 128), F32)
    sum_out = jnp.zeros((32, 128), F32)
    sum_bias = jnp.zeros((8, 128), F32)
    for g in range(2):
        sum_out = sum_out + fold(nt(gpre[g * 128 : (g + 1) * 128, :], hid[g * 256 : (g + 1) * 256, :]))
    for g in range(2):
        mlp_backward(g)
    for g in range(2):
        by_in = nt(field[g * 128 : g * 128 + 128 + ONES, :], slope[g * 256 : (g + 1) * 256, :])
        sum_in = sum_in + fold(by_in[g * ONES : g * ONES + 128])
        sum_bias = sum_bias + fold(by_in[(1 - g) * 128 : (1 - g) * 128 + 8])
    lane32 = lax.broadcasted_iota(jnp.int32, (32, 128), 1)
    asend[...] = jnp.where(lane32 < 64, sum_in, pltpu.roll(sum_out, 64, 1)).astype(BF16)
    absend[...] = sum_bias
    gather_start(4, "depth", asend, arecv)
    gather_start(7, "depth", absend, abrecv)

    eta_wait(2, recvs.at[2])
    zg = eta_forward(recvs.at[2])
    for ri in range(2):
        zbuf[ri] = zg[:, ri * 128 : (ri + 1) * 128]
    br, bi = mix(rt2, -1.0)
    eta_inverse(br, bi, sends.at[3])
    eta_start(3, sends.at[3], recvs.at[3])

    dsend[:, :, 64:128] = zg.T.reshape(4, 64, 64)
    mb = drecv.shape[2]

    for peer in dep_peers:
        pltpu.make_async_remote_copy(
            src_ref=dsend.at[:, pl.ds(pl.multiple_of(peer * mb, mb), mb), :],
            dst_ref=drecv.at[dep],
            send_sem=send_sem.at[5],
            recv_sem=recv_sem.at[5],
            device_id=(peer, eta),
            device_id_type=MESH,
        ).start()
    drecv[dep] = dsend[:, pl.ds(pl.multiple_of(dep * mb, mb), mb), :]

    mlp_to_input(0)
    blocks_wait(recv_sem.at[4], arecv, n_dep)
    blocks_wait(recv_sem.at[7], abrecv, n_dep)
    mine = arecv[0].astype(F32)
    bias = abrecv[0]
    for i in range(1, n_dep):
        mine = mine + arecv[i].astype(F32)
        bias = bias + abrecv[i]
    bsend[...] = mine.astype(BF16)
    bbsend[...] = bias
    gather_start(6, "eta", bsend, brecv)
    gather_start(8, "eta", bbsend, bbrecv)
    mlp_to_input(1)

    blocks_wait(recv_sem.at[5], drecv, n_dep)
    got = drecv[...].reshape(256, 128)
    lane = lax.broadcasted_iota(jnp.int32, (256, 128), 1)
    row_c = lax.rem(lax.broadcasted_iota(jnp.int32, (128, 1024), 0), 32)
    repeat = (row_c == lax.broadcasted_iota(jnp.int32, (128, 1024), 1) // 32).astype(F32).astype(BF16)
    row_o = lax.rem(lax.broadcasted_iota(jnp.int32, (128, 128), 0), 32)
    tiled = (row_o == lax.rem(lax.broadcasted_iota(jnp.int32, (128, 128), 1), 32)).astype(F32).astype(BF16)
    for d in range(2):
        xexp[d] = nn(jnp.where(lane // 32 == d, got, 0.0).astype(BF16), repeat)
        gexp[d] = nn(jnp.where(lane // 32 == 2 + d, got, 0.0).astype(BF16), tiled)
    for kk in range(2):
        for t in range(8):
            lanes = slice(t * 128, (t + 1) * 128)
            real = jnp.zeros((mb, 128), F32)
            imag = jnp.zeros((mb, 128), F32)
            for i in range(n_dep):
                r0 = (i * 4 + kk) * mb
                r1 = (i * 4 + 2 + kk) * mb
                for d in range(2):
                    xr = xexp[d, r0 : r0 + mb, lanes]
                    xi = xexp[d, r1 : r1 + mb, lanes]
                    gr = gexp[d, r0 : r0 + mb, :]
                    gi = gexp[d, r1 : r1 + mb, :]
                    real = real + (xr * gr + xi * gi)
                    imag = imag + (xr * gi - xi * gr)
            gspec[0, kk, :, lanes] = real * factor
            gspec[1, kk, :, lanes] = imag * factor

    eta_wait(3, recvs.at[3])
    phi_inverse_lhs(recvs.at[3])

    blocks_wait(recv_sem.at[6], brecv, n_eta)
    blocks_wait(recv_sem.at[8], bbrecv, n_eta)
    sums = brecv[0].astype(F32)
    bias = bbrecv[0]
    for i in range(1, n_eta):
        sums = sums + brecv[i].astype(F32)
        bias = bias + bbrecv[i]
    sums = sums * norm
    out_in[...] = sums[:, 0:64]
    out_out[...] = pltpu.roll(sums, 64, 1)[:, 0:64]
    out_bias[...] = (bias * norm)[0:1, 0:64]

    for n in range(4):
        eta_sent(n, sends.at[n])
    blocks_wait(send_sem.at[4], arecv, n_dep)
    blocks_wait(send_sem.at[5], drecv, n_dep)
    blocks_wait(send_sem.at[6], brecv, n_eta)
    blocks_wait(send_sem.at[7], abrecv, n_dep)
    blocks_wait(send_sem.at[8], bbrecv, n_eta)


def finish(chunk, part, w_all, tinv, *refs):
    ins, (gin, *outs), total, sem = refs[:4], refs[4:9], refs[9], refs[10]
    copies = [pltpu.make_async_copy(src, dst, sem.at[n]) for n, (src, dst) in enumerate(zip(ins, outs))]
    for copy in copies:
        copy.start()
    for i in range(part.shape[1] // chunk):
        cols = pl.ds(i * chunk, chunk)
        total[:, cols] = part[:, cols] + nn(w_all[...], tinv[:, cols])
        copy = pltpu.make_async_copy(total.at[:, cols], gin.at[:, cols], sem.at[4 + i])
        copy.start()
        copies.append(copy)
    for copy in copies:
        copy.wait()


def local(n_dep, n_eta, field_in, grad_out, spectral_weight, mlp_in, mlp_bias, mlp_out):
    layers, cells, chans, n_phi = field_in.shape
    owned, n_modes = spectral_weight.shape[1:3]
    n_cells = cells * n_eta
    assert (layers, cells, chans, owned, n_modes) == (2, 4, 32, 2, 64)
    fwd, inv = phi_table(n_phi, owned * n_eta)
    efwd, einv = eta_tables(n_cells, n_modes, n_eta)
    rows = layers * cells * chans
    mb = n_modes // n_dep
    chunk, out_chunk = min(CHUNK, n_phi), min(OUT_CHUNK, n_phi)
    factor = math.sqrt(n_phi * n_cells / (owned * n_eta * n_modes))
    norm = 1.0 / math.sqrt(layers * n_dep * n_cells * n_phi)
    vmem = pl.BlockSpec(memory_space=pltpu.VMEM)
    hbm = pl.BlockSpec(memory_space=pltpu.HBM)
    scratch = [
        pltpu.VMEM((rows + ONES, n_phi), BF16),
        pltpu.VMEM((rows, n_phi), BF16),
        pltpu.VMEM((4 * n_modes, 1024), BF16),
        pltpu.VMEM(fwd.shape, BF16),
        pltpu.VMEM(efwd.shape, BF16),
        pltpu.VMEM(einv.shape, BF16),
        pltpu.VMEM((2 * rows, n_phi), BF16),
        pltpu.VMEM((2 * rows, n_phi), BF16),
        pltpu.VMEM((rows, n_phi), BF16),
        pltpu.VMEM((256, 128), BF16),
        pltpu.VMEM((128, 256), BF16),
        pltpu.VMEM((128, 256), BF16),
        pltpu.VMEM((256, 128), BF16),
        pltpu.VMEM((256, 128), F32),
        pltpu.VMEM((2, 1024, 128), F32),
        pltpu.VMEM((2, 1024, 128), F32),
        pltpu.VMEM((2, 64, 128), F32),
        pltpu.VMEM((32, 64), BF16),
        pltpu.VMEM((1, 64), F32),
        pltpu.VMEM((32, 64), BF16),
        pltpu.VMEM((4, 8 * n_eta, 128), F32),
        pltpu.VMEM((4, 8 * n_eta, 128), F32),
        pltpu.VMEM((4, 64, 128), F32),
        pltpu.VMEM((n_dep, 4, mb, 128), F32),
        pltpu.VMEM((2, 256, 1024), F32),
        pltpu.VMEM((2, 256, 128), F32),
        pltpu.VMEM((32, 128), BF16),
        pltpu.VMEM((n_dep, 32, 128), BF16),
        pltpu.VMEM((32, 128), BF16),
        pltpu.VMEM((n_eta, 32, 128), BF16),
        pltpu.VMEM((8, 128), F32),
        pltpu.VMEM((n_dep, 8, 128), F32),
        pltpu.VMEM((8, 128), F32),
        pltpu.VMEM((n_eta, 8, 128), F32),
        pltpu.SemaphoreType.DMA((11,)),
        pltpu.SemaphoreType.DMA((9,)),
        pltpu.SemaphoreType.DMA((9,)),
    ]
    sizes = ((rows, n_phi), (2, 2, mb, 1024), (32, 64), (32, 64), (1, 64))
    passed = [pltpu.VMEM((rows, n_phi), F32), pltpu.VMEM((rows, 4 * n_eta), BF16), pltpu.VMEM(inv.shape, BF16)]
    passed += [pltpu.VMEM(size, F32) for size in sizes[1:]]
    operands = (
        field_in.reshape(rows, n_phi),
        grad_out.reshape(rows, n_phi),
        spectral_weight.reshape(4 * n_modes, 1024),
        mlp_in,
        mlp_bias.reshape(1, 64),
        mlp_out.T,
        jnp.asarray(fwd),
        jnp.asarray(inv),
        jnp.asarray(efwd),
        jnp.asarray(einv),
    )
    results = pl.pallas_call(
        functools.partial(kernel, n_dep, n_eta, chunk, factor, norm),
        out_shape=tuple(passed),
        in_specs=[hbm] * 10,
        out_specs=(vmem,) * 7,
        scratch_shapes=scratch,
        compiler_params=pltpu.CompilerParams(
            collective_id=0, has_side_effects=True, vmem_limit_bytes=48 * 1024 * 1024
        ),
    )(*(pltpu.with_memory_space_constraint(x, pltpu.HBM) for x in operands))
    gin, gspec, g_in, g_outt, g_bias = pl.pallas_call(
        functools.partial(finish, out_chunk),
        out_shape=tuple(jax.ShapeDtypeStruct(size, F32) for size in sizes),
        in_specs=[vmem] * 7,
        out_specs=(hbm,) * 5,
        scratch_shapes=[
            pltpu.VMEM((rows, n_phi), F32),
            pltpu.SemaphoreType.DMA((4 + n_phi // out_chunk,)),
        ],
    )(*(pltpu.with_memory_space_constraint(x, pltpu.VMEM) for x in results))
    return gin.reshape(layers, cells, chans, n_phi), gspec, g_in, g_outt.T, g_bias.reshape(64)


def solution(mesh):
    return jax.shard_map(
        functools.partial(local, mesh.shape["depth"], mesh.shape["eta"]),
        mesh=mesh,
        in_specs=(
            P("depth", "eta", None, None),
            P("depth", "eta", None, None),
            P(None, "eta", None, None),
            P(),
            P(),
            P(),
        ),
        out_specs=(P("depth", "eta", None, None), P(None, "eta", "depth", None), P(), P(), P()),
        check_vma=False,
    )
```

```python
import functools
import math

import jax
import jax.numpy as jnp
import ml_dtypes
import numpy as np
from jax import lax
from jax.experimental import pallas as pl
from jax.experimental.pallas import tpu as pltpu
from jax.sharding import PartitionSpec as P

F32 = jnp.float32
BF16 = jnp.bfloat16
MESH = pl.DeviceIdType.MESH
CHUNK = 2048


def bf(table):
    return table.astype(np.float32).astype(ml_dtypes.bfloat16)


def phi_table(n_phi, n_modes):
    owners = n_modes // 2
    mode = 2 * np.arange(owners)[None, :] + np.arange(2)[:, None]
    freq = np.where(mode < n_modes // 2, mode, n_phi - n_modes + mode)
    theta = 2.0 * np.pi / n_phi * ((freq[:, :, None] * np.arange(n_phi)) % n_phi)
    pairs = np.stack([np.cos(theta), -np.sin(theta)], axis=1).reshape(4 * owners, n_phi)
    return bf(pairs / math.sqrt(n_phi)), bf(pairs / math.sqrt(n_modes))


def eta_tables(n_eta, n_modes, owners):
    j, hi, lo = np.meshgrid(np.arange(owners), np.arange(2), np.arange(2), indexing="ij")
    cell = 4 * j + 2 * hi + lo
    phase = 2.0 * np.pi / n_eta * ((cell[..., None] * np.arange(n_modes)) % n_eta)
    cosine, sine = np.cos(phase), np.sin(phase)
    fwd = np.zeros((2, owners, 2, 2, 2, 2, 2, n_modes))
    inv = np.zeros((owners, 2, 2, 2, 2, 2, 2, n_modes))
    for low in range(2):
        c, s = cosine[:, :, low], sine[:, :, low]
        for kk in range(2):
            fwd[low, :, kk, 0, :, 0, kk] = c
            fwd[low, :, kk, 1, :, 0, kk] = s
            fwd[low, :, kk, 0, :, 1, kk] = -s
            fwd[low, :, kk, 1, :, 1, kk] = c
            inv[:, kk, 0, :, low, 0, kk] = c
            inv[:, kk, 0, :, low, 1, kk] = -s
            inv[:, kk, 1, :, low, 0, kk] = s
            inv[:, kk, 1, :, low, 1, kk] = c
    fwd = fwd.reshape(2 * 8 * owners, 4 * n_modes) / math.sqrt(n_eta)
    inv = inv.reshape(8 * owners, 8 * n_modes) / math.sqrt(n_modes)
    return bf(fwd), bf(inv)


def far_first(n_eta):
    if n_eta != 32:
        return [(s,) for s in range(1, n_eta)]
    steps = [(x, z, y) for x in range(4) for z in range(2) for y in range(4)]
    return sorted(steps[1:], key=lambda s: -(min(s[0], 4 - s[0]) + s[1] + min(s[2], 4 - s[2])))


def eta_peer(eta, n_eta, step):
    if len(step) == 1:
        return lax.rem(eta + step[0], n_eta)
    x, z, y = eta // 8, lax.rem(eta // 4, 2), lax.rem(eta, 4)
    return lax.rem(x + step[0], 4) * 8 + lax.rem(z + step[1], 2) * 4 + lax.rem(y + step[2], 4)


def nn(a, b):
    return lax.dot_general(a, b, (((1,), (0,)), ((), ())), preferred_element_type=F32)


def nt(a, b):
    return lax.dot_general(a, b, (((1,), (1,)), ((), ())), preferred_element_type=F32)


def cdf_and_density(v):
    cdf = 0.5 + 0.5 * lax.erf(v * (1.0 / math.sqrt(2.0)))
    density = jnp.exp(-0.5 * v * v) * (1.0 / math.sqrt(2.0 * math.pi))
    return cdf, density


ONES = 16


def field_rows(d):
    return slice(d * (128 + ONES), d * (128 + ONES) + 128)


def eta_order(x, gap=0):
    blocks = [x[b * 32 + b // 4 * gap : (b + 1) * 32 + b // 4 * gap] for b in range(8)]
    return jnp.concatenate([blocks[d * 4 + hi * 2 + lo] for hi in range(2) for lo in range(2) for d in range(2)], axis=0)


def cell_order(x):
    blocks = [x[b * 32 : (b + 1) * 32] for b in range(8)]
    return jnp.concatenate([blocks[hi * 4 + lo * 2 + d] for d in range(2) for hi in range(2) for lo in range(2)], axis=0)


def kernel(
    n_dep,
    n_eta,
    chunk,
    factor,
    norm,
    field_hbm,
    cotan_hbm,
    weight_hbm,
    mlp_in_hbm,
    mlp_bias_hbm,
    mlp_outt_hbm,
    fwd_hbm,
    inv_hbm,
    efwd_hbm,
    einv_hbm,
    part,
    gspec,
    out_in,
    out_out,
    out_bias,
    field,
    cotan,
    weight,
    tfwd,
    tinv,
    efwd,
    einv,
    hid,
    slope,
    gpre,
    w_all,
    m_up,
    m_down,
    m_outt,
    m_out,
    bias_col,
    rt,
    rt2,
    zbuf,
    mlp_in,
    mlp_bias,
    mlp_outt,
    sends,
    recvs,
    xsend,
    xrecv,
    gsend,
    grecv,
    xexp,
    gexp,
    asend,
    arecv,
    bsend,
    brecv,
    absend,
    abrecv,
    bbsend,
    bbrecv,
    load_sem,
    send_sem,
    recv_sem,
):
    dep = lax.axis_index("depth")
    eta = lax.axis_index("eta")
    n_phi = field.shape[1]
    n_chunks = n_phi // chunk
    mb = xrecv.shape[2]

    barrier = pltpu.get_barrier_semaphore()

    eta_peers = [eta_peer(eta, n_eta, step) for step in far_first(n_eta)]
    dep_peers = [lax.rem(dep + s, n_dep) for s in range(1, n_dep)]
    for peer in eta_peers:
        pl.semaphore_signal(barrier, inc=1, device_id=(dep, peer), device_id_type=MESH)
    for peer in dep_peers:
        pl.semaphore_signal(barrier, inc=1, device_id=(peer, eta), device_id_type=MESH)

    loads = [
        pltpu.make_async_copy(src, dst, load_sem.at[n])
        for n, (src, dst) in enumerate(
            (
                (field_hbm.at[pl.ds(0, 128)], field.at[pl.ds(0, 128)]),
                (field_hbm.at[pl.ds(128, 128)], field.at[pl.ds(128 + ONES, 128)]),
                (fwd_hbm, tfwd),
                (efwd_hbm, efwd),
                (einv_hbm, einv),
                (weight_hbm, weight),
                (inv_hbm, tinv),
                (cotan_hbm, cotan),
                (mlp_in_hbm, mlp_in),
                (mlp_bias_hbm, mlp_bias),
                (mlp_outt_hbm, mlp_outt),
            )
        )
    ]
    for copy in loads:
        copy.start()
    field[128 : 128 + ONES, :] = jnp.ones((ONES, n_phi), BF16)

    def eta_start(n, send, recv):
        for peer in eta_peers:
            pltpu.make_async_remote_copy(
                src_ref=send.at[pl.ds(pl.multiple_of(peer * 8, 8), 8)],
                dst_ref=recv.at[pl.ds(pl.multiple_of(eta * 8, 8), 8)],
                send_sem=send_sem.at[n],
                recv_sem=recv_sem.at[n],
                device_id=(dep, peer),
                device_id_type=MESH,
            ).start()
        own = pl.ds(pl.multiple_of(eta * 8, 8), 8)
        recv[own, :] = send[own, :]

    def eta_wait(n, recv):
        rows = pl.ds(0, 8 * (n_eta - 1))
        pltpu.make_async_copy(recv.at[rows], recv.at[rows], recv_sem.at[n]).wait()

    def eta_sent(n, send):
        rows = pl.ds(0, 8 * (n_eta - 1))
        pltpu.make_async_copy(send.at[rows], send.at[rows], send_sem.at[n]).wait()

    def gather_start(n, axis, block, recv):
        me, peers = (dep, dep_peers) if axis == "depth" else (eta, eta_peers)
        for peer in peers:
            pltpu.make_async_remote_copy(
                src_ref=block,
                dst_ref=recv.at[me],
                send_sem=send_sem.at[n],
                recv_sem=recv_sem.at[n],
                device_id=(peer, eta) if axis == "depth" else (dep, peer),
                device_id_type=MESH,
            ).start()
        recv[me] = block[...]

    def blocks_wait(sem, recv, count):
        some = pl.ds(0, count - 1)
        pltpu.make_async_copy(recv.at[some], recv.at[some], sem).wait()

    def modes_start(n, z, send, recv):
        for ri in range(2):
            part_z = z[:, ri * 128 : (ri + 1) * 128]
            send[ri] = jnp.concatenate([part_z, pltpu.roll(part_z, 64, 1)], axis=0).T[0:64]
        for peer in dep_peers:
            pltpu.make_async_remote_copy(
                src_ref=send.at[:, pl.ds(pl.multiple_of(peer * mb, mb), mb), :],
                dst_ref=recv.at[dep],
                send_sem=send_sem.at[n],
                recv_sem=recv_sem.at[n],
                device_id=(peer, eta),
                device_id_type=MESH,
            ).start()
        recv[dep] = send[:, pl.ds(pl.multiple_of(dep * mb, mb), mb), :]

    def phi_forward(x, send, gap=0):
        spectra = nt(tfwd[...], eta_order(x, gap))
        for q in range(4):
            for hi in range(2):
                send[pl.ds(q * 2 + hi, n_eta, stride=8), :] = spectra[
                    q * n_eta : (q + 1) * n_eta, hi * 128 : (hi + 1) * 128
                ]

    def eta_forward(recv):
        xt = recv[...].T.astype(BF16)
        half = 8 * n_eta
        return nn(xt[0:64], efwd[0:half, :]) + nn(xt[64:128], efwd[half:, :])

    def eta_inverse(real, imag, send):
        v = jnp.concatenate([real, imag], axis=1).astype(BF16)
        zero = jnp.zeros_like(v)
        both = jnp.concatenate(
            [jnp.concatenate([v, zero], axis=1), jnp.concatenate([zero, v], axis=1)], axis=0
        )
        send[...] = nt(einv[...], both)

    def phi_inverse_lhs(recv):
        halves = []
        for hi in range(2):
            rows = [recv[pl.ds(q * 2 + hi, n_eta, stride=8), :] for q in range(4)]
            halves.append(jnp.concatenate(rows, axis=0).T)
        w_all[...] = cell_order(jnp.concatenate(halves, axis=0)).astype(BF16)

    for copy in loads[:3]:
        copy.wait()
    phi_forward(field[...], sends.at[0], ONES)
    pl.semaphore_wait(barrier, n_eta + n_dep - 2)
    eta_start(0, sends.at[0], recvs.at[0])

    for copy in loads[8:]:
        copy.wait()

    def tile_rows(x):
        return jnp.concatenate([x] * 4, axis=0)

    spread = (
        lax.broadcasted_iota(jnp.int32, (64, 256), 0) == lax.rem(lax.broadcasted_iota(jnp.int32, (64, 256), 1), 64)
    ).astype(F32).astype(BF16)
    keep = (
        lax.broadcasted_iota(jnp.int32, (128, 256), 0) // 32 == lax.broadcasted_iota(jnp.int32, (128, 256), 1) // 64
    )
    for matrix, wide, tall in ((mlp_in, m_down, m_up), (mlp_outt, m_outt, m_out)):
        four = jnp.where(keep, tile_rows(nn(matrix[...], spread)), 0.0)
        wide[...] = four.astype(BF16)
        tall[...] = four.T.astype(BF16)
    diagonal = lax.broadcasted_iota(jnp.int32, (64, 64), 0) == lax.broadcasted_iota(jnp.int32, (64, 64), 1)
    column = jnp.sum(jnp.where(diagonal, mlp_bias[...], 0.0), axis=1, keepdims=True)
    bias_col[...] = jnp.broadcast_to(tile_rows(column), (256, 128))

    def mlp_forward(g):
        def body(i):
            cols = pl.ds(i * chunk, chunk)
            pre = nn(m_up[...], field[field_rows(g), cols])
            pre = pre + jnp.concatenate([bias_col[...]] * (chunk // 128), axis=1)
            cdf, density = cdf_and_density(pre)
            hidden = (pre * cdf).astype(BF16)
            hid[g * 256 : (g + 1) * 256, cols] = hidden
            slope[g * 256 : (g + 1) * 256, cols] = (cdf + pre * density).astype(BF16)
            part[g * 128 : (g + 1) * 128, cols] = nn(m_outt[...], hidden)

        for i in range(n_chunks):
            body(i)

    loads[5].wait()
    for ri in range(2):
        rt[ri] = weight[ri * 128 : (ri + 1) * 128, :].astype(F32).T
    mlp_forward(0)

    loads[3].wait()
    loads[4].wait()
    eta_wait(0, recvs.at[0])
    zx = eta_forward(recvs.at[0])
    for ri in range(2):
        zbuf[ri] = zx[:, ri * 128 : (ri + 1) * 128]

    def mix(table, conjugate):
        real = [jnp.zeros((32, 128), F32) for _ in range(2)]
        imag = [jnp.zeros((32, 128), F32) for _ in range(2)]
        for c in range(32):
            wr = table[0, c * 32 : (c + 1) * 32, :]
            wi = table[1, c * 32 : (c + 1) * 32, :]
            for d in range(2):
                zr = zbuf[0, d * 32 + c : d * 32 + c + 1, :]
                zi = zbuf[1, d * 32 + c : d * 32 + c + 1, :]
                if conjugate:
                    real[d] = real[d] + zr * wr + zi * wi
                    imag[d] = imag[d] + zi * wr - zr * wi
                else:
                    real[d] = real[d] + zr * wr - zi * wi
                    imag[d] = imag[d] + zi * wr + zr * wi
        return jnp.concatenate(real, axis=0), jnp.concatenate(imag, axis=0)

    vr, vi = mix(rt, False)
    eta_inverse(vr, vi, sends.at[1])
    eta_start(1, sends.at[1], recvs.at[1])

    modes_start(9, zx, xsend, xrecv)
    mlp_forward(1)
    for ri in range(2):
        for o in range(32):
            rt2[ri, o * 32 : (o + 1) * 32, :] = rt[ri, pl.ds(o, 32, stride=32), :]

    loads[6].wait()
    loads[7].wait()
    eta_wait(1, recvs.at[1])
    phi_inverse_lhs(recvs.at[1])

    def pre_chunk(i):
        cols = pl.ds(i * chunk, chunk)
        pre = nn(w_all[...], tinv[:, cols]) + part[:, cols]
        cdf, density = cdf_and_density(pre)
        grad = (cotan[:, cols].astype(F32) * (cdf + pre * density)).astype(BF16)
        gpre[:, cols] = grad

    for i in range(n_chunks):
        pre_chunk(i)
    phi_forward(gpre[...], sends.at[2])
    eta_start(2, sends.at[2], recvs.at[2])

    def mlp_backward(g):
        def body(i):
            cols = pl.ds(i * chunk, chunk)
            grad = nn(m_out[...], gpre[g * 128 : (g + 1) * 128, cols])
            slope[g * 256 : (g + 1) * 256, cols] = (
                grad * slope[g * 256 : (g + 1) * 256, cols].astype(F32)
            ).astype(BF16)

        for i in range(n_chunks):
            body(i)

    def mlp_to_input(g):
        def body(i):
            cols = pl.ds(i * chunk, chunk)
            rows = slice(g * 128, (g + 1) * 128)
            part[rows, cols] = cotan[rows, cols].astype(F32) + nn(
                m_down[...], slope[g * 256 : (g + 1) * 256, cols]
            )

        for i in range(n_chunks):
            body(i)

    def fold(x):
        rows = x.shape[0] // 4 if x.shape[0] > 8 else 0
        acc = None
        for a in range(4):
            tile = x[a * rows : a * rows + (rows or 8), (a // 2) * 128 : (a // 2 + 1) * 128]
            tile = pltpu.roll(tile, 64, 1) if a % 2 else tile
            acc = tile if acc is None else acc + tile
        return acc

    sum_in = jnp.zeros((32, 128), F32)
    sum_out = jnp.zeros((32, 128), F32)
    sum_bias = jnp.zeros((8, 128), F32)
    for g in range(2):
        sum_out = sum_out + fold(nt(gpre[g * 128 : (g + 1) * 128, :], hid[g * 256 : (g + 1) * 256, :]))
    for g in range(2):
        mlp_backward(g)
    for g in range(2):
        by_in = nt(field[g * 128 : g * 128 + 128 + ONES, :], slope[g * 256 : (g + 1) * 256, :])
        sum_in = sum_in + fold(by_in[g * ONES : g * ONES + 128])
        sum_bias = sum_bias + fold(by_in[(1 - g) * 128 : (1 - g) * 128 + 8])
    lane32 = lax.broadcasted_iota(jnp.int32, (32, 128), 1)
    asend[...] = jnp.where(lane32 < 64, sum_in, pltpu.roll(sum_out, 64, 1)).astype(BF16)
    absend[...] = sum_bias[0:1]
    gather_start(4, "depth", asend, arecv)
    gather_start(7, "depth", absend, abrecv)

    blocks_wait(recv_sem.at[9], xrecv, n_dep)
    got = xrecv[...].reshape(128, 128)
    lane = lax.broadcasted_iota(jnp.int32, (128, 128), 1)
    row_c = lax.rem(lax.broadcasted_iota(jnp.int32, (128, 1024), 0), 32)
    repeat = (row_c == lax.broadcasted_iota(jnp.int32, (128, 1024), 1) // 32).astype(F32).astype(BF16)
    for b in range(4):
        xexp[b] = nn(jnp.where(lane // 32 == b, got, 0.0).astype(BF16), repeat)

    eta_wait(2, recvs.at[2])
    zg = eta_forward(recvs.at[2])
    for ri in range(2):
        zbuf[ri] = zg[:, ri * 128 : (ri + 1) * 128]
    br, bi = mix(rt2, True)
    eta_inverse(br, bi, sends.at[3])
    eta_start(3, sends.at[3], recvs.at[3])

    modes_start(5, zg, gsend, grecv)
    blocks_wait(recv_sem.at[4], arecv, n_dep)
    blocks_wait(recv_sem.at[7], abrecv, n_dep)
    mine = arecv[0].astype(F32)
    bias = abrecv[0]
    for i in range(1, n_dep):
        mine = mine + arecv[i].astype(F32)
        bias = bias + abrecv[i]
    bsend[...] = mine.astype(BF16)
    bbsend[...] = bias
    gather_start(6, "eta", bsend, brecv)
    gather_start(8, "eta", bbsend, bbrecv)
    for g in range(2):
        mlp_to_input(g)

    blocks_wait(recv_sem.at[5], grecv, n_dep)
    got = grecv[...].reshape(128, 128)
    row_o = lax.rem(lax.broadcasted_iota(jnp.int32, (128, 128), 0), 32)
    tiled = (row_o == lax.rem(lax.broadcasted_iota(jnp.int32, (128, 128), 1), 32)).astype(F32).astype(BF16)
    for b in range(4):
        gexp[b] = nn(jnp.where(lane // 32 == b, got, 0.0).astype(BF16), tiled)
    for kk in range(2):
        for t in range(8):
            lanes = slice(t * 128, (t + 1) * 128)
            real = jnp.zeros((mb, 128), F32)
            imag = jnp.zeros((mb, 128), F32)
            for i in range(n_dep):
                r0 = i * 2 * mb
                r1 = r0 + mb
                for d in range(2):
                    b = kk * 2 + d
                    xr = xexp[b, r0 : r0 + mb, lanes]
                    xi = xexp[b, r1 : r1 + mb, lanes]
                    gr = gexp[b, r0 : r0 + mb, :]
                    gi = gexp[b, r1 : r1 + mb, :]
                    real = real + (xr * gr + xi * gi)
                    imag = imag + (xr * gi - xi * gr)
            gspec[0, kk, :, lanes] = real * factor
            gspec[1, kk, :, lanes] = imag * factor

    eta_wait(3, recvs.at[3])
    phi_inverse_lhs(recvs.at[3])
    part[...] = part[...] + nn(w_all[...], tinv[...])

    blocks_wait(recv_sem.at[6], brecv, n_eta)
    blocks_wait(recv_sem.at[8], bbrecv, n_eta)
    sums = brecv[0].astype(F32)
    bias = bbrecv[0]
    for i in range(1, n_eta):
        sums = sums + brecv[i].astype(F32)
        bias = bias + bbrecv[i]
    sums = sums * norm
    out_in[...] = sums[:, 0:64]
    out_out[...] = pltpu.roll(sums, 64, 1)[:, 0:64]
    out_bias[...] = (bias * norm)[:, 0:64]

    for n in range(4):
        eta_sent(n, sends.at[n])
    blocks_wait(send_sem.at[4], arecv, n_dep)
    blocks_wait(send_sem.at[5], grecv, n_dep)
    blocks_wait(send_sem.at[9], xrecv, n_dep)
    blocks_wait(send_sem.at[6], brecv, n_eta)
    blocks_wait(send_sem.at[7], abrecv, n_dep)
    blocks_wait(send_sem.at[8], bbrecv, n_eta)


def write_out(*refs):
    ins, outs, sem = refs[:5], refs[5:10], refs[10]
    copies = [pltpu.make_async_copy(src, dst, sem.at[n]) for n, (src, dst) in enumerate(zip(ins, outs))]
    for copy in copies:
        copy.start()
    for copy in copies:
        copy.wait()


def local(n_dep, n_eta, field_in, grad_out, spectral_weight, mlp_in, mlp_bias, mlp_out):
    layers, cells, chans, n_phi = field_in.shape
    owned, n_modes = spectral_weight.shape[1:3]
    n_cells = cells * n_eta
    assert (layers, cells, chans, owned, n_modes) == (2, 4, 32, 2, 64)
    fwd, inv = phi_table(n_phi, owned * n_eta)
    efwd, einv = eta_tables(n_cells, n_modes, n_eta)
    rows = layers * cells * chans
    mb = n_modes // n_dep
    chunk = min(CHUNK, n_phi)
    factor = math.sqrt(n_phi * n_cells / (owned * n_eta * n_modes))
    norm = 1.0 / math.sqrt(layers * n_dep * n_cells * n_phi)
    vmem = pl.BlockSpec(memory_space=pltpu.VMEM)
    hbm = pl.BlockSpec(memory_space=pltpu.HBM)
    scratch = [
        pltpu.VMEM((rows + ONES, n_phi), BF16),
        pltpu.VMEM((rows, n_phi), BF16),
        pltpu.VMEM((4 * n_modes, 1024), BF16),
        pltpu.VMEM(fwd.shape, BF16),
        pltpu.VMEM(inv.shape, BF16),
        pltpu.VMEM(efwd.shape, BF16),
        pltpu.VMEM(einv.shape, BF16),
        pltpu.VMEM((2 * rows, n_phi), BF16),
        pltpu.VMEM((2 * rows, n_phi), BF16),
        pltpu.VMEM((rows, n_phi), BF16),
        pltpu.VMEM((rows, 4 * n_eta), BF16),
        pltpu.VMEM((256, 128), BF16),
        pltpu.VMEM((128, 256), BF16),
        pltpu.VMEM((128, 256), BF16),
        pltpu.VMEM((256, 128), BF16),
        pltpu.VMEM((256, 128), F32),
        pltpu.VMEM((2, 1024, 128), F32),
        pltpu.VMEM((2, 1024, 128), F32),
        pltpu.VMEM((2, 64, 128), F32),
        pltpu.VMEM((32, 64), BF16),
        pltpu.VMEM((1, 64), F32),
        pltpu.VMEM((32, 64), BF16),
        pltpu.VMEM((4, 8 * n_eta, 128), F32),
        pltpu.VMEM((4, 8 * n_eta, 128), F32),
        pltpu.VMEM((2, 64, 128), F32),
        pltpu.VMEM((n_dep, 2, mb, 128), F32),
        pltpu.VMEM((2, 64, 128), F32),
        pltpu.VMEM((n_dep, 2, mb, 128), F32),
        pltpu.VMEM((4, 128, 1024), F32),
        pltpu.VMEM((4, 128, 128), F32),
        pltpu.VMEM((32, 128), BF16),
        pltpu.VMEM((n_dep, 32, 128), BF16),
        pltpu.VMEM((32, 128), BF16),
        pltpu.VMEM((n_eta, 32, 128), BF16),
        pltpu.VMEM((1, 128), F32),
        pltpu.VMEM((n_dep, 1, 128), F32),
        pltpu.VMEM((1, 128), F32),
        pltpu.VMEM((n_eta, 1, 128), F32),
        pltpu.SemaphoreType.DMA((11,)),
        pltpu.SemaphoreType.DMA((10,)),
        pltpu.SemaphoreType.DMA((10,)),
    ]
    sizes = ((rows, n_phi), (2, 2, mb, 1024), (32, 64), (32, 64), (1, 64))
    operands = (
        field_in.reshape(rows, n_phi),
        grad_out.reshape(rows, n_phi),
        spectral_weight.reshape(4 * n_modes, 1024),
        mlp_in,
        mlp_bias.reshape(1, 64),
        mlp_out.T,
        jnp.asarray(fwd),
        jnp.asarray(inv),
        jnp.asarray(efwd),
        jnp.asarray(einv),
    )
    results = pl.pallas_call(
        functools.partial(kernel, n_dep, n_eta, chunk, factor, norm),
        out_shape=tuple(pltpu.VMEM(size, F32) for size in sizes),
        in_specs=[hbm] * 10,
        out_specs=(vmem,) * 5,
        scratch_shapes=scratch,
        compiler_params=pltpu.CompilerParams(
            collective_id=0, has_side_effects=True, vmem_limit_bytes=48 * 1024 * 1024
        ),
    )(*(pltpu.with_memory_space_constraint(x, pltpu.HBM) for x in operands))
    gin, gspec, g_in, g_outt, g_bias = pl.pallas_call(
        write_out,
        out_shape=tuple(jax.ShapeDtypeStruct(size, F32) for size in sizes),
        in_specs=[vmem] * 5,
        out_specs=(hbm,) * 5,
        scratch_shapes=[pltpu.SemaphoreType.DMA((5,))],
    )(*(pltpu.with_memory_space_constraint(x, pltpu.VMEM) for x in results))
    return gin.reshape(layers, cells, chans, n_phi), gspec, g_in, g_outt.T, g_bias.reshape(64)


def solution(mesh):
    return jax.shard_map(
        functools.partial(local, mesh.shape["depth"], mesh.shape["eta"]),
        mesh=mesh,
        in_specs=(
            P("depth", "eta", None, None),
            P("depth", "eta", None, None),
            P(None, "eta", None, None),
            P(),
            P(),
            P(),
        ),
        out_specs=(P("depth", "eta", None, None), P(None, "eta", "depth", None), P(), P(), P()),
        check_vma=False,
    )
```

```python
import functools
import math

import jax
import jax.numpy as jnp
import ml_dtypes
import numpy as np
from jax import lax
from jax.experimental import pallas as pl
from jax.experimental.pallas import tpu as pltpu
from jax.sharding import PartitionSpec as P

F32 = jnp.float32
BF16 = jnp.bfloat16
MESH = pl.DeviceIdType.MESH
CHUNK = 2048


def bf(table):
    return table.astype(np.float32).astype(ml_dtypes.bfloat16)


def phi_table(n_phi, n_modes):
    owners = n_modes // 2
    mode = 2 * np.arange(owners)[None, :] + np.arange(2)[:, None]
    freq = np.where(mode < n_modes // 2, mode, n_phi - n_modes + mode)
    theta = 2.0 * np.pi / n_phi * ((freq[:, :, None] * np.arange(n_phi)) % n_phi)
    pairs = np.stack([np.cos(theta), -np.sin(theta)], axis=1).reshape(4 * owners, n_phi)
    return bf(pairs / math.sqrt(n_phi)), bf(pairs / math.sqrt(n_modes))


def eta_tables(n_eta, n_modes, owners):
    j, hi, lo = np.meshgrid(np.arange(owners), np.arange(2), np.arange(2), indexing="ij")
    cell = 4 * j + 2 * hi + lo
    phase = 2.0 * np.pi / n_eta * ((cell[..., None] * np.arange(n_modes)) % n_eta)
    cosine, sine = np.cos(phase), np.sin(phase)
    fwd = np.zeros((2, owners, 2, 2, 2, 2, 2, n_modes))
    inv = np.zeros((owners, 2, 2, 2, 2, 2, 2, n_modes))
    for low in range(2):
        c, s = cosine[:, :, low], sine[:, :, low]
        for kk in range(2):
            fwd[low, :, kk, 0, :, 0, kk] = c
            fwd[low, :, kk, 1, :, 0, kk] = s
            fwd[low, :, kk, 0, :, 1, kk] = -s
            fwd[low, :, kk, 1, :, 1, kk] = c
            inv[:, kk, 0, :, low, 0, kk] = c
            inv[:, kk, 0, :, low, 1, kk] = -s
            inv[:, kk, 1, :, low, 0, kk] = s
            inv[:, kk, 1, :, low, 1, kk] = c
    fwd = fwd.reshape(2 * 8 * owners, 4 * n_modes) / math.sqrt(n_eta)
    inv = inv.reshape(8 * owners, 8 * n_modes) / math.sqrt(n_modes)
    return bf(fwd), bf(inv)


def far_first(n_x, n_z):
    steps = [(x, z, y) for x in range(n_x) for z in range(n_z) for y in range(4)]
    return sorted(steps[1:], key=lambda s: -(min(s[0], n_x - s[0]) + s[1] + min(s[2], 4 - s[2])))


def eta_peer(eta, n_x, step):
    x, z, y = eta // 8, lax.rem(eta // 4, 2), lax.rem(eta, 4)
    return lax.rem(x + step[0], n_x) * 8 + lax.rem(z + step[1], 2) * 4 + lax.rem(y + step[2], 4)


def nn(a, b):
    return lax.dot_general(a, b, (((1,), (0,)), ((), ())), preferred_element_type=F32)


def nt(a, b):
    return lax.dot_general(a, b, (((1,), (1,)), ((), ())), preferred_element_type=F32)


def cdf_and_density(v):
    cdf = 0.5 + 0.5 * lax.erf(v * (1.0 / math.sqrt(2.0)))
    density = jnp.exp(-0.5 * v * v) * (1.0 / math.sqrt(2.0 * math.pi))
    return cdf, density


ONES = 16


def field_rows(d):
    return slice(d * (128 + ONES), d * (128 + ONES) + 128)


def eta_order(x, gap=0):
    blocks = [x[b * 32 + b // 4 * gap : (b + 1) * 32 + b // 4 * gap] for b in range(8)]
    return jnp.concatenate([blocks[d * 4 + hi * 2 + lo] for hi in range(2) for lo in range(2) for d in range(2)], axis=0)


def cell_order(x):
    blocks = [x[b * 32 : (b + 1) * 32] for b in range(8)]
    return jnp.concatenate([blocks[hi * 4 + lo * 2 + d] for d in range(2) for hi in range(2) for lo in range(2)], axis=0)


def kernel(
    n_dep,
    n_eta,
    chunk,
    factor,
    norm,
    field_hbm,
    cotan_hbm,
    weight_hbm,
    mlp_in_hbm,
    mlp_bias_hbm,
    mlp_outt_hbm,
    fwd_hbm,
    inv_hbm,
    efwd_hbm,
    einv_hbm,
    part,
    gspec,
    out_in,
    out_out,
    out_bias,
    field,
    cotan,
    weight,
    tfwd,
    tinv,
    efwd,
    einv,
    hid,
    slope,
    gpre,
    w_all,
    m_up,
    m_down,
    m_outt,
    m_out,
    bias_col,
    rt,
    rt2,
    zbuf,
    mlp_in,
    mlp_bias,
    mlp_outt,
    sends,
    recvs,
    xsend,
    xrecv,
    gsend,
    grecv,
    xexp,
    gexp,
    asend,
    arecv,
    bsend,
    brecv,
    absend,
    abrecv,
    bbsend,
    bbrecv,
    load_sem,
    send_sem,
    recv_sem,
):
    dep = lax.axis_index("depth")
    eta = lax.axis_index("eta")
    n_phi = field.shape[1]
    n_chunks = n_phi // chunk
    mb = xrecv.shape[2]

    barrier = pltpu.get_barrier_semaphore()

    n_x = n_eta // 8
    eta_peers = [eta_peer(eta, n_x, step) for step in far_first(n_x, 2)]
    dep_peers = [lax.rem(dep + s, n_dep) for s in sorted(range(1, n_dep), key=lambda s: abs(s - n_dep // 2))]
    other = eta_peer(eta, n_x, (0, 1, 0))
    line = [(peer, e) for peer in dep_peers for e in (other, eta)] + [(dep, other)]
    line_place = dep * 2 + lax.rem(eta // 4, 2)
    plane = [(dep, eta_peer(eta, n_x, step)) for step in far_first(n_x, 1)]
    plane_place = eta // 8 * 4 + lax.rem(eta, 4)
    for peer in eta_peers:
        pl.semaphore_signal(barrier, inc=1, device_id=(dep, peer), device_id_type=MESH)
    for peer in line[:-1]:
        pl.semaphore_signal(barrier, inc=1, device_id=peer, device_id_type=MESH)
    loads = [
        pltpu.make_async_copy(src, dst, load_sem.at[n])
        for n, (src, dst) in enumerate(
            (
                (field_hbm.at[pl.ds(0, 128)], field.at[pl.ds(0, 128)]),
                (field_hbm.at[pl.ds(128, 128)], field.at[pl.ds(128 + ONES, 128)]),
                (fwd_hbm, tfwd),
                (efwd_hbm, efwd),
                (einv_hbm, einv),
                (weight_hbm, weight),
                (inv_hbm, tinv),
                (cotan_hbm, cotan),
                (mlp_in_hbm, mlp_in),
                (mlp_bias_hbm, mlp_bias),
                (mlp_outt_hbm, mlp_outt),
            )
        )
    ]
    for copy in loads:
        copy.start()
    field[128 : 128 + ONES, :] = jnp.ones((ONES, n_phi), BF16)

    def eta_start(n, send, recv):
        for peer in eta_peers:
            pltpu.make_async_remote_copy(
                src_ref=send.at[pl.ds(pl.multiple_of(peer * 8, 8), 8)],
                dst_ref=recv.at[pl.ds(pl.multiple_of(eta * 8, 8), 8)],
                send_sem=send_sem.at[n],
                recv_sem=recv_sem.at[n],
                device_id=(dep, peer),
                device_id_type=MESH,
            ).start()
        own = pl.ds(pl.multiple_of(eta * 8, 8), 8)
        recv[own, :] = send[own, :]

    def eta_wait(n, recv):
        rows = pl.ds(0, 8 * (n_eta - 1))
        pltpu.make_async_copy(recv.at[rows], recv.at[rows], recv_sem.at[n]).wait()

    def eta_sent(n, send):
        rows = pl.ds(0, 8 * (n_eta - 1))
        pltpu.make_async_copy(send.at[rows], send.at[rows], send_sem.at[n]).wait()

    def gather_start(n, place, peers, block, recv):
        for peer in peers:
            pltpu.make_async_remote_copy(
                src_ref=block,
                dst_ref=recv.at[place],
                send_sem=send_sem.at[n],
                recv_sem=recv_sem.at[n],
                device_id=peer,
                device_id_type=MESH,
            ).start()
        recv[place] = block[...]

    def blocks_wait(sem, recv, count):
        some = pl.ds(0, count - 1)
        pltpu.make_async_copy(recv.at[some], recv.at[some], sem).wait()

    def modes_start(n, z, send, recv):
        for ri in range(2):
            part_z = z[:, ri * 128 : (ri + 1) * 128]
            send[ri] = jnp.concatenate([part_z, pltpu.roll(part_z, 64, 1)], axis=0).T[0:64]
        for peer in dep_peers:
            pltpu.make_async_remote_copy(
                src_ref=send.at[:, pl.ds(pl.multiple_of(peer * mb, mb), mb), :],
                dst_ref=recv.at[dep],
                send_sem=send_sem.at[n],
                recv_sem=recv_sem.at[n],
                device_id=(peer, eta),
                device_id_type=MESH,
            ).start()
        recv[dep] = send[:, pl.ds(pl.multiple_of(dep * mb, mb), mb), :]

    def phi_forward(x, send, gap=0):
        spectra = nt(tfwd[...], eta_order(x, gap))
        for q in range(4):
            for hi in range(2):
                send[pl.ds(q * 2 + hi, n_eta, stride=8), :] = spectra[
                    q * n_eta : (q + 1) * n_eta, hi * 128 : (hi + 1) * 128
                ]

    def eta_forward(recv):
        xt = recv[...].T.astype(BF16)
        half = 8 * n_eta
        return nn(xt[0:64], efwd[0:half, :]) + nn(xt[64:128], efwd[half:, :])

    def eta_inverse(real, imag, send):
        v = jnp.concatenate([real, imag], axis=1).astype(BF16)
        zero = jnp.zeros_like(v)
        both = jnp.concatenate(
            [jnp.concatenate([v, zero], axis=1), jnp.concatenate([zero, v], axis=1)], axis=0
        )
        send[...] = nt(einv[...], both)

    def phi_inverse_lhs(recv):
        halves = []
        for hi in range(2):
            rows = [recv[pl.ds(q * 2 + hi, n_eta, stride=8), :] for q in range(4)]
            halves.append(jnp.concatenate(rows, axis=0).T)
        w_all[...] = cell_order(jnp.concatenate(halves, axis=0)).astype(BF16)

    for copy in loads[:3]:
        copy.wait()
    phi_forward(field[...], sends.at[0], ONES)
    pl.semaphore_wait(barrier, n_eta - 1 + 2 * (n_dep - 1))
    eta_start(0, sends.at[0], recvs.at[0])

    for copy in loads[8:]:
        copy.wait()

    def tile_rows(x):
        return jnp.concatenate([x] * 4, axis=0)

    spread = (
        lax.broadcasted_iota(jnp.int32, (64, 256), 0) == lax.rem(lax.broadcasted_iota(jnp.int32, (64, 256), 1), 64)
    ).astype(F32).astype(BF16)
    keep = (
        lax.broadcasted_iota(jnp.int32, (128, 256), 0) // 32 == lax.broadcasted_iota(jnp.int32, (128, 256), 1) // 64
    )
    for matrix, wide, tall in ((mlp_in, m_down, m_up), (mlp_outt, m_outt, m_out)):
        four = jnp.where(keep, tile_rows(nn(matrix[...], spread)), 0.0)
        wide[...] = four.astype(BF16)
        tall[...] = four.T.astype(BF16)
    diagonal = lax.broadcasted_iota(jnp.int32, (64, 64), 0) == lax.broadcasted_iota(jnp.int32, (64, 64), 1)
    column = jnp.sum(jnp.where(diagonal, mlp_bias[...], 0.0), axis=1, keepdims=True)
    bias_col[...] = jnp.broadcast_to(tile_rows(column), (256, 128))

    def mlp_forward(g):
        def body(i):
            cols = pl.ds(i * chunk, chunk)
            pre = nn(m_up[...], field[field_rows(g), cols])
            pre = pre + jnp.concatenate([bias_col[...]] * (chunk // 128), axis=1)
            cdf, density = cdf_and_density(pre)
            hidden = (pre * cdf).astype(BF16)
            hid[g * 256 : (g + 1) * 256, cols] = hidden
            slope[g * 256 : (g + 1) * 256, cols] = (cdf + pre * density).astype(BF16)
            part[g * 128 : (g + 1) * 128, cols] = nn(m_outt[...], hidden)

        for i in range(n_chunks):
            body(i)

    loads[5].wait()
    for ri in range(2):
        rt[ri] = weight[ri * 128 : (ri + 1) * 128, :].astype(F32).T
    mlp_forward(0)

    loads[3].wait()
    loads[4].wait()
    eta_wait(0, recvs.at[0])
    zx = eta_forward(recvs.at[0])
    for ri in range(2):
        zbuf[ri] = zx[:, ri * 128 : (ri + 1) * 128]

    def mix(table, conjugate):
        real = [jnp.zeros((32, 128), F32) for _ in range(2)]
        imag = [jnp.zeros((32, 128), F32) for _ in range(2)]
        for c in range(32):
            wr = table[0, c * 32 : (c + 1) * 32, :]
            wi = table[1, c * 32 : (c + 1) * 32, :]
            for d in range(2):
                zr = zbuf[0, d * 32 + c : d * 32 + c + 1, :]
                zi = zbuf[1, d * 32 + c : d * 32 + c + 1, :]
                if conjugate:
                    real[d] = real[d] + (zr * wr + zi * wi)
                    imag[d] = imag[d] + (zi * wr - zr * wi)
                else:
                    real[d] = real[d] + (zr * wr - zi * wi)
                    imag[d] = imag[d] + (zi * wr + zr * wi)
        return jnp.concatenate(real, axis=0), jnp.concatenate(imag, axis=0)

    vr, vi = mix(rt, False)
    eta_inverse(vr, vi, sends.at[1])
    eta_start(1, sends.at[1], recvs.at[1])

    modes_start(9, zx, xsend, xrecv)
    mlp_forward(1)
    for ri in range(2):
        for o in range(32):
            rt2[ri, o * 32 : (o + 1) * 32, :] = rt[ri, pl.ds(o, 32, stride=32), :]

    loads[6].wait()
    loads[7].wait()
    eta_wait(1, recvs.at[1])
    phi_inverse_lhs(recvs.at[1])

    def pre_chunk(i):
        cols = pl.ds(i * chunk, chunk)
        pre = nn(w_all[...], tinv[:, cols]) + part[:, cols]
        cdf, density = cdf_and_density(pre)
        grad = (cotan[:, cols].astype(F32) * (cdf + pre * density)).astype(BF16)
        gpre[:, cols] = grad

    for i in range(n_chunks):
        pre_chunk(i)
    phi_forward(gpre[...], sends.at[2])
    eta_start(2, sends.at[2], recvs.at[2])

    def mlp_backward(g):
        def body(i):
            cols = pl.ds(i * chunk, chunk)
            grad = nn(m_out[...], gpre[g * 128 : (g + 1) * 128, cols])
            slope[g * 256 : (g + 1) * 256, cols] = (
                grad * slope[g * 256 : (g + 1) * 256, cols].astype(F32)
            ).astype(BF16)

        for i in range(n_chunks):
            body(i)

    def mlp_to_input(g):
        def body(i):
            cols = pl.ds(i * chunk, chunk)
            rows = slice(g * 128, (g + 1) * 128)
            part[rows, cols] = cotan[rows, cols].astype(F32) + nn(
                m_down[...], slope[g * 256 : (g + 1) * 256, cols]
            )

        for i in range(n_chunks):
            body(i)

    def fold(x):
        rows = x.shape[0] // 4 if x.shape[0] > 8 else 0
        acc = None
        for a in range(4):
            tile = x[a * rows : a * rows + (rows or 8), (a // 2) * 128 : (a // 2 + 1) * 128]
            tile = pltpu.roll(tile, 64, 1) if a % 2 else tile
            acc = tile if acc is None else acc + tile
        return acc

    sum_in = jnp.zeros((32, 128), F32)
    sum_out = jnp.zeros((32, 128), F32)
    sum_bias = jnp.zeros((8, 128), F32)
    for g in range(2):
        sum_out = sum_out + fold(nt(gpre[g * 128 : (g + 1) * 128, :], hid[g * 256 : (g + 1) * 256, :]))
    for g in range(2):
        mlp_backward(g)
    for g in range(2):
        by_in = nt(field[g * 128 : g * 128 + 128 + ONES, :], slope[g * 256 : (g + 1) * 256, :])
        sum_in = sum_in + fold(by_in[g * ONES : g * ONES + 128])
        sum_bias = sum_bias + fold(by_in[(1 - g) * 128 : (1 - g) * 128 + 8])
    lane32 = lax.broadcasted_iota(jnp.int32, (32, 128), 1)
    asend[...] = jnp.where(lane32 < 64, sum_in, pltpu.roll(sum_out, 64, 1)).astype(BF16)
    absend[...] = sum_bias[0:1]
    gather_start(4, line_place, line, asend, arecv)
    gather_start(7, line_place, line, absend, abrecv)

    blocks_wait(recv_sem.at[9], xrecv, n_dep)
    got = xrecv[...].reshape(128, 128)
    lane = lax.broadcasted_iota(jnp.int32, (128, 128), 1)
    row_c = lax.rem(lax.broadcasted_iota(jnp.int32, (128, 1024), 0), 32)
    repeat = (row_c == lax.broadcasted_iota(jnp.int32, (128, 1024), 1) // 32).astype(F32).astype(BF16)
    for b in range(4):
        xexp[b] = nn(jnp.where(lane // 32 == b, got, 0.0).astype(BF16), repeat)

    eta_wait(2, recvs.at[2])
    zg = eta_forward(recvs.at[2])
    for ri in range(2):
        zbuf[ri] = zg[:, ri * 128 : (ri + 1) * 128]
    br, bi = mix(rt2, True)
    eta_inverse(br, bi, sends.at[3])
    eta_start(3, sends.at[3], recvs.at[3])

    modes_start(5, zg, gsend, grecv)
    blocks_wait(recv_sem.at[4], arecv, 2 * n_dep)
    blocks_wait(recv_sem.at[7], abrecv, 2 * n_dep)
    mine = arecv[0].astype(F32)
    bias = abrecv[0]
    for i in range(1, 2 * n_dep):
        mine = mine + arecv[i].astype(F32)
        bias = bias + abrecv[i]
    bsend[...] = mine.astype(BF16)
    bbsend[...] = bias
    gather_start(6, plane_place, plane, bsend, brecv)
    gather_start(8, plane_place, plane, bbsend, bbrecv)
    for g in range(2):
        mlp_to_input(g)

    blocks_wait(recv_sem.at[5], grecv, n_dep)
    got = grecv[...].reshape(128, 128)
    row_o = lax.rem(lax.broadcasted_iota(jnp.int32, (128, 128), 0), 32)
    tiled = (row_o == lax.rem(lax.broadcasted_iota(jnp.int32, (128, 128), 1), 32)).astype(F32).astype(BF16)
    for b in range(4):
        gexp[b] = nn(jnp.where(lane // 32 == b, got, 0.0).astype(BF16), tiled)
    for kk in range(2):
        for t in range(8):
            lanes = slice(t * 128, (t + 1) * 128)
            real = jnp.zeros((mb, 128), F32)
            imag = jnp.zeros((mb, 128), F32)
            for i in range(n_dep):
                r0 = i * 2 * mb
                r1 = r0 + mb
                for d in range(2):
                    b = kk * 2 + d
                    xr = xexp[b, r0 : r0 + mb, lanes]
                    xi = xexp[b, r1 : r1 + mb, lanes]
                    gr = gexp[b, r0 : r0 + mb, :]
                    gi = gexp[b, r1 : r1 + mb, :]
                    real = real + (xr * gr + xi * gi)
                    imag = imag + (xr * gi - xi * gr)
            gspec[0, kk, :, lanes] = real * factor
            gspec[1, kk, :, lanes] = imag * factor

    eta_wait(3, recvs.at[3])
    phi_inverse_lhs(recvs.at[3])
    part[...] = part[...] + nn(w_all[...], tinv[...])

    blocks_wait(recv_sem.at[6], brecv, n_eta // 2)
    blocks_wait(recv_sem.at[8], bbrecv, n_eta // 2)
    sums = brecv[0].astype(F32)
    bias = bbrecv[0]
    for i in range(1, n_eta // 2):
        sums = sums + brecv[i].astype(F32)
        bias = bias + bbrecv[i]
    sums = sums * norm
    out_in[...] = sums[:, 0:64]
    out_out[...] = pltpu.roll(sums, 64, 1)[:, 0:64]
    out_bias[...] = (bias * norm)[:, 0:64]

    for n in range(4):
        eta_sent(n, sends.at[n])
    blocks_wait(send_sem.at[4], arecv, 2 * n_dep)
    blocks_wait(send_sem.at[5], grecv, n_dep)
    blocks_wait(send_sem.at[9], xrecv, n_dep)
    blocks_wait(send_sem.at[6], brecv, n_eta // 2)
    blocks_wait(send_sem.at[7], abrecv, 2 * n_dep)
    blocks_wait(send_sem.at[8], bbrecv, n_eta // 2)


def write_out(*refs):
    ins, outs, sem = refs[:5], refs[5:10], refs[10]
    copies = [pltpu.make_async_copy(src, dst, sem.at[n]) for n, (src, dst) in enumerate(zip(ins, outs))]
    for copy in copies:
        copy.start()
    for copy in copies:
        copy.wait()


def local(n_dep, n_eta, field_in, grad_out, spectral_weight, mlp_in, mlp_bias, mlp_out):
    layers, cells, chans, n_phi = field_in.shape
    owned, n_modes = spectral_weight.shape[1:3]
    n_cells = cells * n_eta
    assert (layers, cells, chans, owned, n_modes) == (2, 4, 32, 2, 64)
    fwd, inv = phi_table(n_phi, owned * n_eta)
    efwd, einv = eta_tables(n_cells, n_modes, n_eta)
    rows = layers * cells * chans
    mb = n_modes // n_dep
    chunk = min(CHUNK, n_phi)
    factor = math.sqrt(n_phi * n_cells / (owned * n_eta * n_modes))
    norm = 1.0 / math.sqrt(layers * n_dep * n_cells * n_phi)
    vmem = pl.BlockSpec(memory_space=pltpu.VMEM)
    hbm = pl.BlockSpec(memory_space=pltpu.HBM)
    scratch = [
        pltpu.VMEM((rows + ONES, n_phi), BF16),
        pltpu.VMEM((rows, n_phi), BF16),
        pltpu.VMEM((4 * n_modes, 1024), BF16),
        pltpu.VMEM(fwd.shape, BF16),
        pltpu.VMEM(inv.shape, BF16),
        pltpu.VMEM(efwd.shape, BF16),
        pltpu.VMEM(einv.shape, BF16),
        pltpu.VMEM((2 * rows, n_phi), BF16),
        pltpu.VMEM((2 * rows, n_phi), BF16),
        pltpu.VMEM((rows, n_phi), BF16),
        pltpu.VMEM((rows, 4 * n_eta), BF16),
        pltpu.VMEM((256, 128), BF16),
        pltpu.VMEM((128, 256), BF16),
        pltpu.VMEM((128, 256), BF16),
        pltpu.VMEM((256, 128), BF16),
        pltpu.VMEM((256, 128), F32),
        pltpu.VMEM((2, 1024, 128), F32),
        pltpu.VMEM((2, 1024, 128), F32),
        pltpu.VMEM((2, 64, 128), F32),
        pltpu.VMEM((32, 64), BF16),
        pltpu.VMEM((1, 64), F32),
        pltpu.VMEM((32, 64), BF16),
        pltpu.VMEM((4, 8 * n_eta, 128), F32),
        pltpu.VMEM((4, 8 * n_eta, 128), F32),
        pltpu.VMEM((2, 64, 128), F32),
        pltpu.VMEM((n_dep, 2, mb, 128), F32),
        pltpu.VMEM((2, 64, 128), F32),
        pltpu.VMEM((n_dep, 2, mb, 128), F32),
        pltpu.VMEM((4, 128, 1024), F32),
        pltpu.VMEM((4, 128, 128), F32),
        pltpu.VMEM((32, 128), BF16),
        pltpu.VMEM((2 * n_dep, 32, 128), BF16),
        pltpu.VMEM((32, 128), BF16),
        pltpu.VMEM((n_eta // 2, 32, 128), BF16),
        pltpu.VMEM((1, 128), F32),
        pltpu.VMEM((2 * n_dep, 1, 128), F32),
        pltpu.VMEM((1, 128), F32),
        pltpu.VMEM((n_eta // 2, 1, 128), F32),
        pltpu.SemaphoreType.DMA((11,)),
        pltpu.SemaphoreType.DMA((10,)),
        pltpu.SemaphoreType.DMA((10,)),
    ]
    sizes = ((rows, n_phi), (2, 2, mb, 1024), (32, 64), (32, 64), (1, 64))
    operands = (
        field_in.reshape(rows, n_phi),
        grad_out.reshape(rows, n_phi),
        spectral_weight.reshape(4 * n_modes, 1024),
        mlp_in,
        mlp_bias.reshape(1, 64),
        mlp_out.T,
        jnp.asarray(fwd),
        jnp.asarray(inv),
        jnp.asarray(efwd),
        jnp.asarray(einv),
    )
    results = pl.pallas_call(
        functools.partial(kernel, n_dep, n_eta, chunk, factor, norm),
        out_shape=tuple(pltpu.VMEM(size, F32) for size in sizes),
        in_specs=[hbm] * 10,
        out_specs=(vmem,) * 5,
        scratch_shapes=scratch,
        compiler_params=pltpu.CompilerParams(
            collective_id=0, has_side_effects=True, vmem_limit_bytes=48 * 1024 * 1024
        ),
    )(*(pltpu.with_memory_space_constraint(x, pltpu.HBM) for x in operands))
    gin, gspec, g_in, g_outt, g_bias = pl.pallas_call(
        write_out,
        out_shape=tuple(jax.ShapeDtypeStruct(size, F32) for size in sizes),
        in_specs=[vmem] * 5,
        out_specs=(hbm,) * 5,
        scratch_shapes=[pltpu.SemaphoreType.DMA((5,))],
    )(*(pltpu.with_memory_space_constraint(x, pltpu.VMEM) for x in results))
    return gin.reshape(layers, cells, chans, n_phi), gspec, g_in, g_outt.T, g_bias.reshape(64)


def solution(mesh):
    return jax.shard_map(
        functools.partial(local, mesh.shape["depth"], mesh.shape["eta"]),
        mesh=mesh,
        in_specs=(
            P("depth", "eta", None, None),
            P("depth", "eta", None, None),
            P(None, "eta", None, None),
            P(),
            P(),
            P(),
        ),
        out_specs=(P("depth", "eta", None, None), P(None, "eta", "depth", None), P(), P(), P()),
        check_vma=False,
    )
```

```python
import functools
import math

import jax
import jax.numpy as jnp
import ml_dtypes
import numpy as np
from jax import lax
from jax.experimental import pallas as pl
from jax.experimental.pallas import tpu as pltpu
from jax.sharding import PartitionSpec as P

F32 = jnp.float32
BF16 = jnp.bfloat16
MESH = pl.DeviceIdType.MESH
CHUNK = 2048


def bf(table):
    return table.astype(np.float32).astype(ml_dtypes.bfloat16)


def phi_table(n_phi, n_modes):
    owners = n_modes // 2
    mode = 2 * np.arange(owners)[None, :] + np.arange(2)[:, None]
    freq = np.where(mode < n_modes // 2, mode, n_phi - n_modes + mode)
    theta = 2.0 * np.pi / n_phi * ((freq[:, :, None] * np.arange(n_phi)) % n_phi)
    pairs = np.stack([np.cos(theta), -np.sin(theta)], axis=1).reshape(4 * owners, n_phi)
    return bf(pairs / math.sqrt(n_phi)), bf(pairs / math.sqrt(n_modes))


def eta_tables(n_eta, n_modes, owners):
    j, hi, lo = np.meshgrid(np.arange(owners), np.arange(2), np.arange(2), indexing="ij")
    cell = 4 * j + 2 * hi + lo
    phase = 2.0 * np.pi / n_eta * ((cell[..., None] * np.arange(n_modes)) % n_eta)
    cosine, sine = np.cos(phase), np.sin(phase)
    fwd = np.zeros((2, owners, 2, 2, 2, 2, 2, n_modes))
    inv = np.zeros((owners, 2, 2, 2, 2, 2, 2, n_modes))
    for low in range(2):
        c, s = cosine[:, :, low], sine[:, :, low]
        for kk in range(2):
            fwd[low, :, kk, 0, :, 0, kk] = c
            fwd[low, :, kk, 1, :, 0, kk] = s
            fwd[low, :, kk, 0, :, 1, kk] = -s
            fwd[low, :, kk, 1, :, 1, kk] = c
            inv[:, kk, 0, :, low, 0, kk] = c
            inv[:, kk, 0, :, low, 1, kk] = -s
            inv[:, kk, 1, :, low, 0, kk] = s
            inv[:, kk, 1, :, low, 1, kk] = c
    fwd = fwd.reshape(2 * 8 * owners, 4 * n_modes) / math.sqrt(n_eta)
    inv = inv.reshape(8 * owners, 8 * n_modes) / math.sqrt(n_modes)
    return bf(fwd), bf(inv)


def far_first(n_x, n_z):
    steps = [(x, z, y) for x in range(n_x) for z in range(n_z) for y in range(4)]
    return sorted(steps[1:], key=lambda s: -(min(s[0], n_x - s[0]) + s[1] + min(s[2], 4 - s[2])))


def eta_peer(eta, n_x, step):
    x, z, y = eta // 8, lax.rem(eta // 4, 2), lax.rem(eta, 4)
    return lax.rem(x + step[0], n_x) * 8 + lax.rem(z + step[1], 2) * 4 + lax.rem(y + step[2], 4)


def nn(a, b):
    return lax.dot_general(a, b, (((1,), (0,)), ((), ())), preferred_element_type=F32)


def nt(a, b):
    return lax.dot_general(a, b, (((1,), (1,)), ((), ())), preferred_element_type=F32)


def cdf_and_density(v):
    cdf = 0.5 + 0.5 * lax.erf(v * (1.0 / math.sqrt(2.0)))
    density = jnp.exp(-0.5 * v * v) * (1.0 / math.sqrt(2.0 * math.pi))
    return cdf, density


ONES = 16


def field_rows(d):
    return slice(d * (128 + ONES), d * (128 + ONES) + 128)


def eta_order(x, gap=0):
    blocks = [x[b * 32 + b // 4 * gap : (b + 1) * 32 + b // 4 * gap] for b in range(8)]
    return jnp.concatenate([blocks[d * 4 + hi * 2 + lo] for hi in range(2) for lo in range(2) for d in range(2)], axis=0)


def cell_order(x):
    blocks = [x[b * 32 : (b + 1) * 32] for b in range(8)]
    return jnp.concatenate([blocks[hi * 4 + lo * 2 + d] for d in range(2) for hi in range(2) for lo in range(2)], axis=0)


def kernel(
    n_dep,
    n_eta,
    chunk,
    factor,
    norm,
    field_hbm,
    cotan_hbm,
    weight_hbm,
    mlp_in_hbm,
    mlp_bias_hbm,
    mlp_outt_hbm,
    fwd_hbm,
    inv_hbm,
    efwd_hbm,
    einv_hbm,
    part,
    w_all,
    tinv,
    gspec,
    out_in,
    out_out,
    out_bias,
    field,
    cotan,
    weight,
    tfwd,
    efwd,
    einv,
    hid,
    slope,
    gpre,
    m_up,
    m_down,
    m_outt,
    m_out,
    bias_col,
    rt,
    rt2,
    zbuf,
    mlp_in,
    mlp_bias,
    mlp_outt,
    sends,
    recvs,
    xsend,
    xrecv,
    gsend,
    grecv,
    xexp,
    gexp,
    asend,
    arecv,
    bsend,
    brecv,
    absend,
    abrecv,
    bbsend,
    bbrecv,
    load_sem,
    send_sem,
    recv_sem,
):
    dep = lax.axis_index("depth")
    eta = lax.axis_index("eta")
    n_phi = field.shape[1]
    n_chunks = n_phi // chunk
    mb = xrecv.shape[2]

    barrier = pltpu.get_barrier_semaphore()

    n_x = n_eta // 8
    eta_peers = [eta_peer(eta, n_x, step) for step in far_first(n_x, 2)]
    dep_peers = [lax.rem(dep + s, n_dep) for s in sorted(range(1, n_dep), key=lambda s: abs(s - n_dep // 2))]
    other = eta_peer(eta, n_x, (0, 1, 0))
    line = [(peer, e) for peer in dep_peers for e in (other, eta)] + [(dep, other)]
    line_place = dep * 2 + lax.rem(eta // 4, 2)
    plane = [(dep, eta_peer(eta, n_x, step)) for step in far_first(n_x, 1)]
    plane_place = eta // 8 * 4 + lax.rem(eta, 4)
    loads = [
        pltpu.make_async_copy(src, dst, load_sem.at[n])
        for n, (src, dst) in enumerate(
            (
                (field_hbm.at[pl.ds(0, 128)], field.at[pl.ds(0, 128)]),
                (field_hbm.at[pl.ds(128, 128)], field.at[pl.ds(128 + ONES, 128)]),
                (fwd_hbm, tfwd),
                (efwd_hbm, efwd),
                (einv_hbm, einv),
                (weight_hbm, weight),
                (inv_hbm, tinv),
                (cotan_hbm, cotan),
                (mlp_in_hbm, mlp_in),
                (mlp_bias_hbm, mlp_bias),
                (mlp_outt_hbm, mlp_outt),
            )
        )
    ]
    for copy in loads[:3]:
        copy.start()
    for peer in eta_peers:
        pl.semaphore_signal(barrier, inc=1, device_id=(dep, peer), device_id_type=MESH)
    for peer in line[:-1]:
        pl.semaphore_signal(barrier, inc=1, device_id=peer, device_id_type=MESH)
    for copy in loads[3:]:
        copy.start()
    field[128 : 128 + ONES, :] = jnp.ones((ONES, n_phi), BF16)

    def eta_start(n, send, recv):
        for peer in eta_peers:
            pltpu.make_async_remote_copy(
                src_ref=send.at[pl.ds(pl.multiple_of(peer * 8, 8), 8)],
                dst_ref=recv.at[pl.ds(pl.multiple_of(eta * 8, 8), 8)],
                send_sem=send_sem.at[n],
                recv_sem=recv_sem.at[n],
                device_id=(dep, peer),
                device_id_type=MESH,
            ).start()
        own = pl.ds(pl.multiple_of(eta * 8, 8), 8)
        recv[own, :] = send[own, :]

    def eta_wait(n, recv):
        rows = pl.ds(0, 8 * (n_eta - 1))
        pltpu.make_async_copy(recv.at[rows], recv.at[rows], recv_sem.at[n]).wait()

    def eta_sent(n, send):
        rows = pl.ds(0, 8 * (n_eta - 1))
        pltpu.make_async_copy(send.at[rows], send.at[rows], send_sem.at[n]).wait()

    def gather_start(n, place, peers, block, recv):
        for peer in peers:
            pltpu.make_async_remote_copy(
                src_ref=block,
                dst_ref=recv.at[place],
                send_sem=send_sem.at[n],
                recv_sem=recv_sem.at[n],
                device_id=peer,
                device_id_type=MESH,
            ).start()
        recv[place] = block[...]

    def blocks_wait(sem, recv, count):
        some = pl.ds(0, count - 1)
        pltpu.make_async_copy(recv.at[some], recv.at[some], sem).wait()

    def modes_start(n, z, send, recv):
        for ri in range(2):
            part_z = z[:, ri * 128 : (ri + 1) * 128]
            send[ri] = jnp.concatenate([part_z, pltpu.roll(part_z, 64, 1)], axis=0).T[0:64]
        for peer in dep_peers:
            pltpu.make_async_remote_copy(
                src_ref=send.at[:, pl.ds(pl.multiple_of(peer * mb, mb), mb), :],
                dst_ref=recv.at[dep],
                send_sem=send_sem.at[n],
                recv_sem=recv_sem.at[n],
                device_id=(peer, eta),
                device_id_type=MESH,
            ).start()
        recv[dep] = send[:, pl.ds(pl.multiple_of(dep * mb, mb), mb), :]

    def phi_forward(x, send, gap=0):
        spectra = nt(tfwd[...], eta_order(x, gap))
        for q in range(4):
            for hi in range(2):
                send[pl.ds(q * 2 + hi, n_eta, stride=8), :] = spectra[
                    q * n_eta : (q + 1) * n_eta, hi * 128 : (hi + 1) * 128
                ]

    def eta_forward(recv):
        xt = recv[...].T.astype(BF16)
        half = 8 * n_eta
        return nn(xt[0:64], efwd[0:half, :]) + nn(xt[64:128], efwd[half:, :])

    def eta_inverse(real, imag, send):
        v = jnp.concatenate([real, imag], axis=1).astype(BF16)
        zero = jnp.zeros_like(v)
        both = jnp.concatenate(
            [jnp.concatenate([v, zero], axis=1), jnp.concatenate([zero, v], axis=1)], axis=0
        )
        send[...] = nt(einv[...], both)

    def phi_inverse_lhs(recv):
        halves = []
        for hi in range(2):
            rows = [recv[pl.ds(q * 2 + hi, n_eta, stride=8), :] for q in range(4)]
            halves.append(jnp.concatenate(rows, axis=0).T)
        w_all[...] = cell_order(jnp.concatenate(halves, axis=0)).astype(BF16)

    for copy in loads[:3]:
        copy.wait()
    phi_forward(field[...], sends.at[0], ONES)
    pl.semaphore_wait(barrier, n_eta - 1 + 2 * (n_dep - 1))
    eta_start(0, sends.at[0], recvs.at[0])

    for copy in loads[8:]:
        copy.wait()

    def tile_rows(x):
        return jnp.concatenate([x] * 4, axis=0)

    spread = (
        lax.broadcasted_iota(jnp.int32, (64, 256), 0) == lax.rem(lax.broadcasted_iota(jnp.int32, (64, 256), 1), 64)
    ).astype(F32).astype(BF16)
    keep = (
        lax.broadcasted_iota(jnp.int32, (128, 256), 0) // 32 == lax.broadcasted_iota(jnp.int32, (128, 256), 1) // 64
    )
    for matrix, wide, tall in ((mlp_in, m_down, m_up), (mlp_outt, m_outt, m_out)):
        four = jnp.where(keep, tile_rows(nn(matrix[...], spread)), 0.0)
        wide[...] = four.astype(BF16)
        tall[...] = four.T.astype(BF16)
    diagonal = lax.broadcasted_iota(jnp.int32, (64, 64), 0) == lax.broadcasted_iota(jnp.int32, (64, 64), 1)
    column = jnp.sum(jnp.where(diagonal, mlp_bias[...], 0.0), axis=1, keepdims=True)
    bias_col[...] = jnp.broadcast_to(tile_rows(column), (256, 128))

    def mlp_forward(g):
        def body(i):
            cols = pl.ds(i * chunk, chunk)
            pre = nn(m_up[...], field[field_rows(g), cols])
            pre = pre + jnp.concatenate([bias_col[...]] * (chunk // 128), axis=1)
            cdf, density = cdf_and_density(pre)
            hidden = (pre * cdf).astype(BF16)
            hid[g * 256 : (g + 1) * 256, cols] = hidden
            slope[g * 256 : (g + 1) * 256, cols] = (cdf + pre * density).astype(BF16)
            part[g * 128 : (g + 1) * 128, cols] = nn(m_outt[...], hidden)

        for i in range(n_chunks):
            body(i)

    loads[5].wait()
    for ri in range(2):
        rt[ri] = weight[ri * 128 : (ri + 1) * 128, :].astype(F32).T
    mlp_forward(0)

    loads[3].wait()
    loads[4].wait()
    eta_wait(0, recvs.at[0])
    zx = eta_forward(recvs.at[0])
    for ri in range(2):
        zbuf[ri] = zx[:, ri * 128 : (ri + 1) * 128]

    def mix(table, conjugate):
        real = [jnp.zeros((32, 128), F32) for _ in range(2)]
        imag = [jnp.zeros((32, 128), F32) for _ in range(2)]
        for c in range(32):
            wr = table[0, c * 32 : (c + 1) * 32, :]
            wi = table[1, c * 32 : (c + 1) * 32, :]
            for d in range(2):
                zr = zbuf[0, d * 32 + c : d * 32 + c + 1, :]
                zi = zbuf[1, d * 32 + c : d * 32 + c + 1, :]
                if conjugate:
                    real[d] = real[d] + (zr * wr + zi * wi)
                    imag[d] = imag[d] + (zi * wr - zr * wi)
                else:
                    real[d] = real[d] + (zr * wr - zi * wi)
                    imag[d] = imag[d] + (zi * wr + zr * wi)
        return jnp.concatenate(real, axis=0), jnp.concatenate(imag, axis=0)

    vr, vi = mix(rt, False)
    eta_inverse(vr, vi, sends.at[1])
    eta_start(1, sends.at[1], recvs.at[1])

    modes_start(9, zx, xsend, xrecv)
    mlp_forward(1)
    for ri in range(2):
        for o in range(32):
            rt2[ri, o * 32 : (o + 1) * 32, :] = rt[ri, pl.ds(o, 32, stride=32), :]

    loads[6].wait()
    loads[7].wait()
    eta_wait(1, recvs.at[1])
    phi_inverse_lhs(recvs.at[1])

    def pre_chunk(i):
        cols = pl.ds(i * chunk, chunk)
        pre = nn(w_all[...], tinv[:, cols]) + part[:, cols]
        cdf, density = cdf_and_density(pre)
        grad = (cotan[:, cols].astype(F32) * (cdf + pre * density)).astype(BF16)
        gpre[:, cols] = grad

    for i in range(n_chunks):
        pre_chunk(i)
    phi_forward(gpre[...], sends.at[2])
    eta_start(2, sends.at[2], recvs.at[2])

    def mlp_backward(g):
        def body(i):
            cols = pl.ds(i * chunk, chunk)
            grad = nn(m_out[...], gpre[g * 128 : (g + 1) * 128, cols])
            slope[g * 256 : (g + 1) * 256, cols] = (
                grad * slope[g * 256 : (g + 1) * 256, cols].astype(F32)
            ).astype(BF16)

        for i in range(n_chunks):
            body(i)

    def mlp_to_input(g):
        def body(i):
            cols = pl.ds(i * chunk, chunk)
            rows = slice(g * 128, (g + 1) * 128)
            part[rows, cols] = cotan[rows, cols].astype(F32) + nn(
                m_down[...], slope[g * 256 : (g + 1) * 256, cols]
            )

        for i in range(n_chunks):
            body(i)

    def fold(x):
        rows = x.shape[0] // 4 if x.shape[0] > 8 else 0
        acc = None
        for a in range(4):
            tile = x[a * rows : a * rows + (rows or 8), (a // 2) * 128 : (a // 2 + 1) * 128]
            tile = pltpu.roll(tile, 64, 1) if a % 2 else tile
            acc = tile if acc is None else acc + tile
        return acc

    sum_in = jnp.zeros((32, 128), F32)
    sum_out = jnp.zeros((32, 128), F32)
    sum_bias = jnp.zeros((8, 128), F32)
    for g in range(2):
        sum_out = sum_out + fold(nt(gpre[g * 128 : (g + 1) * 128, :], hid[g * 256 : (g + 1) * 256, :]))
    for g in range(2):
        mlp_backward(g)
    for g in range(2):
        by_in = nt(field[g * 128 : g * 128 + 128 + ONES, :], slope[g * 256 : (g + 1) * 256, :])
        sum_in = sum_in + fold(by_in[g * ONES : g * ONES + 128])
        sum_bias = sum_bias + fold(by_in[(1 - g) * 128 : (1 - g) * 128 + 8])
    lane32 = lax.broadcasted_iota(jnp.int32, (32, 128), 1)
    asend[...] = jnp.where(lane32 < 64, sum_in, pltpu.roll(sum_out, 64, 1)).astype(BF16)
    absend[...] = sum_bias[0:1]
    gather_start(4, line_place, line, asend, arecv)
    gather_start(7, line_place, line, absend, abrecv)

    blocks_wait(recv_sem.at[9], xrecv, n_dep)
    got = xrecv[...].reshape(128, 128)
    lane = lax.broadcasted_iota(jnp.int32, (128, 128), 1)
    row_c = lax.rem(lax.broadcasted_iota(jnp.int32, (128, 1024), 0), 32)
    repeat = (row_c == lax.broadcasted_iota(jnp.int32, (128, 1024), 1) // 32).astype(F32).astype(BF16)
    for b in range(4):
        xexp[b] = nn(jnp.where(lane // 32 == b, got, 0.0).astype(BF16), repeat)

    eta_wait(2, recvs.at[2])
    zg = eta_forward(recvs.at[2])
    for ri in range(2):
        zbuf[ri] = zg[:, ri * 128 : (ri + 1) * 128]
    br, bi = mix(rt2, True)
    eta_inverse(br, bi, sends.at[3])
    eta_start(3, sends.at[3], recvs.at[3])

    modes_start(5, zg, gsend, grecv)
    blocks_wait(recv_sem.at[4], arecv, 2 * n_dep)
    blocks_wait(recv_sem.at[7], abrecv, 2 * n_dep)
    mine = arecv[0].astype(F32)
    bias = abrecv[0]
    for i in range(1, 2 * n_dep):
        mine = mine + arecv[i].astype(F32)
        bias = bias + abrecv[i]
    bsend[...] = mine.astype(BF16)
    bbsend[...] = bias
    gather_start(6, plane_place, plane, bsend, brecv)
    gather_start(8, plane_place, plane, bbsend, bbrecv)
    for g in range(2):
        mlp_to_input(g)

    blocks_wait(recv_sem.at[5], grecv, n_dep)
    got = grecv[...].reshape(128, 128)
    row_o = lax.rem(lax.broadcasted_iota(jnp.int32, (128, 128), 0), 32)
    tiled = (row_o == lax.rem(lax.broadcasted_iota(jnp.int32, (128, 128), 1), 32)).astype(F32).astype(BF16)
    for b in range(4):
        gexp[b] = nn(jnp.where(lane // 32 == b, got, 0.0).astype(BF16), tiled)
    for kk in range(2):
        for t in range(8):
            lanes = slice(t * 128, (t + 1) * 128)
            real = jnp.zeros((mb, 128), F32)
            imag = jnp.zeros((mb, 128), F32)
            for i in range(n_dep):
                r0 = i * 2 * mb
                r1 = r0 + mb
                for d in range(2):
                    b = kk * 2 + d
                    xr = xexp[b, r0 : r0 + mb, lanes]
                    xi = xexp[b, r1 : r1 + mb, lanes]
                    gr = gexp[b, r0 : r0 + mb, :]
                    gi = gexp[b, r1 : r1 + mb, :]
                    real = real + (xr * gr + xi * gi)
                    imag = imag + (xr * gi - xi * gr)
            gspec[0, kk, :, lanes] = real * factor
            gspec[1, kk, :, lanes] = imag * factor

    eta_wait(3, recvs.at[3])
    phi_inverse_lhs(recvs.at[3])

    blocks_wait(recv_sem.at[6], brecv, n_eta // 2)
    blocks_wait(recv_sem.at[8], bbrecv, n_eta // 2)
    sums = brecv[0].astype(F32)
    bias = bbrecv[0]
    for i in range(1, n_eta // 2):
        sums = sums + brecv[i].astype(F32)
        bias = bias + bbrecv[i]
    sums = sums * norm
    out_in[...] = sums[:, 0:64]
    out_out[...] = pltpu.roll(sums, 64, 1)[:, 0:64]
    out_bias[...] = (bias * norm)[:, 0:64]

    for n in range(4):
        eta_sent(n, sends.at[n])
    blocks_wait(send_sem.at[4], arecv, 2 * n_dep)
    blocks_wait(send_sem.at[5], grecv, n_dep)
    blocks_wait(send_sem.at[9], xrecv, n_dep)
    blocks_wait(send_sem.at[6], brecv, n_eta // 2)
    blocks_wait(send_sem.at[7], abrecv, 2 * n_dep)
    blocks_wait(send_sem.at[8], bbrecv, n_eta // 2)


def finish(part, w_all, tinv, *refs):
    ins, (gin, *outs), total, sem = refs[:4], refs[4:9], refs[9], refs[10]
    copies = [pltpu.make_async_copy(src, dst, sem.at[n]) for n, (src, dst) in enumerate(zip(ins, outs))]
    for copy in copies:
        copy.start()
    width = part.shape[1] // 4
    for i in range(4):
        cols = pl.ds(i * width, width)
        total[:, cols] = part[:, cols] + nn(w_all[...], tinv[:, cols])
        copy = pltpu.make_async_copy(total.at[:, cols], gin.at[:, cols], sem.at[4 + i])
        copy.start()
        copies.append(copy)
    for copy in copies:
        copy.wait()


def local(n_dep, n_eta, field_in, grad_out, spectral_weight, mlp_in, mlp_bias, mlp_out):
    layers, cells, chans, n_phi = field_in.shape
    owned, n_modes = spectral_weight.shape[1:3]
    n_cells = cells * n_eta
    assert (layers, cells, chans, owned, n_modes) == (2, 4, 32, 2, 64)
    fwd, inv = phi_table(n_phi, owned * n_eta)
    efwd, einv = eta_tables(n_cells, n_modes, n_eta)
    rows = layers * cells * chans
    mb = n_modes // n_dep
    chunk = min(CHUNK, n_phi)
    factor = math.sqrt(n_phi * n_cells / (owned * n_eta * n_modes))
    norm = 1.0 / math.sqrt(layers * n_dep * n_cells * n_phi)
    vmem = pl.BlockSpec(memory_space=pltpu.VMEM)
    hbm = pl.BlockSpec(memory_space=pltpu.HBM)
    scratch = [
        pltpu.VMEM((rows + ONES, n_phi), BF16),
        pltpu.VMEM((rows, n_phi), BF16),
        pltpu.VMEM((4 * n_modes, 1024), BF16),
        pltpu.VMEM(fwd.shape, BF16),
        pltpu.VMEM(efwd.shape, BF16),
        pltpu.VMEM(einv.shape, BF16),
        pltpu.VMEM((2 * rows, n_phi), BF16),
        pltpu.VMEM((2 * rows, n_phi), BF16),
        pltpu.VMEM((rows, n_phi), BF16),
        pltpu.VMEM((256, 128), BF16),
        pltpu.VMEM((128, 256), BF16),
        pltpu.VMEM((128, 256), BF16),
        pltpu.VMEM((256, 128), BF16),
        pltpu.VMEM((256, 128), F32),
        pltpu.VMEM((2, 1024, 128), F32),
        pltpu.VMEM((2, 1024, 128), F32),
        pltpu.VMEM((2, 64, 128), F32),
        pltpu.VMEM((32, 64), BF16),
        pltpu.VMEM((1, 64), F32),
        pltpu.VMEM((32, 64), BF16),
        pltpu.VMEM((4, 8 * n_eta, 128), F32),
        pltpu.VMEM((4, 8 * n_eta, 128), F32),
        pltpu.VMEM((2, 64, 128), F32),
        pltpu.VMEM((n_dep, 2, mb, 128), F32),
        pltpu.VMEM((2, 64, 128), F32),
        pltpu.VMEM((n_dep, 2, mb, 128), F32),
        pltpu.VMEM((4, 128, 1024), F32),
        pltpu.VMEM((4, 128, 128), F32),
        pltpu.VMEM((32, 128), BF16),
        pltpu.VMEM((2 * n_dep, 32, 128), BF16),
        pltpu.VMEM((32, 128), BF16),
        pltpu.VMEM((n_eta // 2, 32, 128), BF16),
        pltpu.VMEM((1, 128), F32),
        pltpu.VMEM((2 * n_dep, 1, 128), F32),
        pltpu.VMEM((1, 128), F32),
        pltpu.VMEM((n_eta // 2, 1, 128), F32),
        pltpu.SemaphoreType.DMA((11,)),
        pltpu.SemaphoreType.DMA((10,)),
        pltpu.SemaphoreType.DMA((10,)),
    ]
    sizes = ((rows, n_phi), (2, 2, mb, 1024), (32, 64), (32, 64), (1, 64))
    passed = [(sizes[0], F32), ((rows, 4 * n_eta), BF16), (inv.shape, BF16)] + [(size, F32) for size in sizes[1:]]
    operands = (
        field_in.reshape(rows, n_phi),
        grad_out.reshape(rows, n_phi),
        spectral_weight.reshape(4 * n_modes, 1024),
        mlp_in,
        mlp_bias.reshape(1, 64),
        mlp_out.T,
        jnp.asarray(fwd),
        jnp.asarray(inv),
        jnp.asarray(efwd),
        jnp.asarray(einv),
    )
    results = pl.pallas_call(
        functools.partial(kernel, n_dep, n_eta, chunk, factor, norm),
        out_shape=tuple(pltpu.VMEM(*spec) for spec in passed),
        in_specs=[hbm] * 10,
        out_specs=(vmem,) * 7,
        scratch_shapes=scratch,
        compiler_params=pltpu.CompilerParams(
            collective_id=0, has_side_effects=True, vmem_limit_bytes=48 * 1024 * 1024
        ),
    )(*(pltpu.with_memory_space_constraint(x, pltpu.HBM) for x in operands))
    gin, gspec, g_in, g_outt, g_bias = pl.pallas_call(
        finish,
        out_shape=tuple(jax.ShapeDtypeStruct(size, F32) for size in sizes),
        in_specs=[vmem] * 7,
        out_specs=(hbm,) * 5,
        scratch_shapes=[pltpu.VMEM((rows, n_phi), F32), pltpu.SemaphoreType.DMA((8,))],
    )(*(pltpu.with_memory_space_constraint(x, pltpu.VMEM) for x in results))
    return gin.reshape(layers, cells, chans, n_phi), gspec, g_in, g_outt.T, g_bias.reshape(64)


def solution(mesh):
    return jax.shard_map(
        functools.partial(local, mesh.shape["depth"], mesh.shape["eta"]),
        mesh=mesh,
        in_specs=(
            P("depth", "eta", None, None),
            P("depth", "eta", None, None),
            P(None, "eta", None, None),
            P(),
            P(),
            P(),
        ),
        out_specs=(P("depth", "eta", None, None), P(None, "eta", "depth", None), P(), P(), P()),
        check_vma=False,
    )
```
